32 devices in a mesh: groups: 2 (over y), wide: 4 (over z), narrow: 4 (over x, core).
Axes of the slice: x: 2, y: 2, z: 4, core: 2. Of those that a mesh axis runs over, the one named last changes fastest.
Arguments:
- tokens: bfloat16 [128, 8192], P(('groups', 'wide'), 'narrow'), parts along dimension 0, may hold values from -60 to 60
- signs: int32 [128, 8192], P(('groups', 'wide'), 'narrow'), parts along dimension 0, may hold values 0 or 1
- magnitude: float32 [128, 8192], P(('groups', 'wide'), 'narrow'), parts along dimension 0, may hold values from 0.05 to 0.5
- target: bfloat16 [128, 8192], P(('groups', 'wide'), 'narrow'), parts along dimension 0, may hold values from -6 to 6
- norm_gain: float32 [8192], P('narrow'), may hold values from 0.1 to 1.9
- gate_weight: bfloat16 [8192, 20480], P('narrow', 'wide'), may hold values from -0.0625 to 0.0625
- up_weight: bfloat16 [8192, 20480], P('narrow', 'wide'), may hold values from -0.0625 to 0.0625
- down_weight: bfloat16 [20480, 8192], P('wide', 'narrow'), may hold values from -0.0390625 to 0.0390625
Outputs:
- new_delta: float32 [128, 8192], P(('groups', 'wide'), 'narrow'), parts along dimension 0
The draws below stay inside these ranges and needn't reach their ends.
There are 2 independent parts, one for each index of `groups`. The reference program is written for one: setup_inputs(seed, part) draws one part's arguments, and reference() takes and returns one part's arrays. A program takes and returns all parts, laid end to end along the dimension named above; an argument that names none is the same for every part. Nothing has to cross between parts.
All inputs are finite; a program needn't handle non-finite values. No bound on the sum of `signs` on one device may be relied on, other than what follows from the above.
Results may differ from the reference program's by a relative error of at most 0.0034.
Values may be sent and summed in bfloat16 or wider, within the bound.
No kernel may reach another device: no remote copies, remote signals or barrier semaphores. Data moves between devices by JAX's collectives and lax.ppermute only.
A program may use at most 192 MiB of HBM per device.

```python
import math
import jax
import jax.numpy as jnp
from jax import lax

D = 8192
FF = 20480
TOKENS = 64


def draw_tokens(key, part):
    keys = jax.random.split(jax.random.fold_in(key, 17), 3)
    pos = jnp.arange(D, dtype=jnp.float32) / D
    col_scale = 0.3 * jnp.exp(math.log(10.0) * (0.6 * pos + 0.4 * jax.random.uniform(keys[1], (D,))))
    row_scale = jnp.exp(jax.random.uniform(keys[0], (TOKENS, 1), minval=math.log(0.3), maxval=math.log(3.0)))
    base = jax.random.normal(keys[2], (TOKENS, D))
    values = jnp.clip(base * row_scale * col_scale, -60.0, 60.0)
    return values.astype(jnp.bfloat16)


def place_ends(entries, stream_key, low, top_value):
    longest = entries.shape.index(max(entries.shape))
    spots = []
    for shift in (0, 1):
        where = [jax.random.randint(jax.random.fold_in(stream_key, axis), (), 0, length) for axis, length in enumerate(entries.shape)]
        where[longest] = (where[longest] + shift) % entries.shape[longest]
        spots.append(tuple(where))
    return entries.at[spots[0]].set(low).at[spots[1]].set(top_value)


def level_of(key, extent, cuts, low, high):
    def one(position, shards_of):
        draws = jax.random.uniform(jax.random.fold_in(jax.random.fold_in(key, 6), position), (shards_of,), jnp.float32, low / len(cuts), high / len(cuts))
        return jnp.repeat(jnp.exp(draws), extent[position] // shards_of).reshape((-1,) + (1,) * (len(extent) - position - 1))

    gain = one(*cuts[0])
    for cut in cuts[1:]:
        gain = gain * one(*cut)
    return gain


def scatter_about(own_key, extent, deviation, most, cuts=(), held_as=jnp.bfloat16):
    level = level_of(own_key, extent, cuts, -0.22, 0.18) if cuts else 1.0
    drawn = jax.random.normal(own_key, extent, jnp.float32) * deviation * level
    return jnp.minimum(jnp.maximum(drawn, -most), most).astype(held_as)


def setup_inputs(seed: int = 0, part: int = 0) -> dict:
    arg_keys = jax.random.split(jax.random.key(seed), 9)
    part_splits = jax.random.split(jax.random.fold_in(arg_keys[8], part), 9)
    return {
        "tokens": draw_tokens(jax.random.fold_in(jax.random.fold_in(arg_keys[8], part), 71), part),
        "signs": place_ends((jax.random.randint(part_splits[1], (TOKENS, D), 0, 2) < 1).astype(jnp.int32), jax.random.fold_in(part_splits[1], 1), 0, 1),
        "magnitude": jnp.clip(jnp.exp(math.log(0.5) - 2.3025851 * jax.random.uniform(part_splits[2], (TOKENS, D), jnp.float32) ** level_of(part_splits[2], (TOKENS, D), ((0, 4), (1, 4)), -0.2, 0.2)), 0.05, 0.5),
        "target": scatter_about(part_splits[3], (TOKENS, D), 1.0, 6.0, ((0, 4), (1, 4))),
        "norm_gain": jnp.clip(1.0 + 0.18 * jax.random.normal(arg_keys[4], (D,), jnp.float32), 0.1, 1.9),
        "gate_weight": scatter_about(arg_keys[5], (D, FF), D ** -0.5, 0.0625, ((0, 4), (1, 4))),
        "up_weight": scatter_about(arg_keys[6], (D, FF), D ** -0.5, 0.0625, ((0, 4), (1, 4))),
        "down_weight": scatter_about(arg_keys[7], (FF, D), FF ** -0.5, 0.0390625, ((0, 4), (1, 4))),
    }


EPS = 1e-05
ASCENT = 0.5

def reference(tokens, signs, magnitude, target, norm_gain, gate_weight, up_weight, down_weight):
    delta = (2 * signs - 1).astype(jnp.float32) * magnitude
    latent = tokens.astype(jnp.float32) + delta
    scale = lax.rsqrt(lax.optimization_barrier(jnp.mean(latent * latent, axis=1, keepdims=True)) + EPS)
    unit = latent * scale
    normed = (unit * norm_gain).astype(jnp.bfloat16)
    gate = jnp.dot(normed, gate_weight, preferred_element_type=jnp.float32)
    up = jnp.dot(normed, up_weight, preferred_element_type=jnp.float32)
    back_hidden = jnp.dot(target, jnp.transpose(down_weight), preferred_element_type=jnp.float32)
    sig = jax.nn.sigmoid(gate)
    back_gate = (back_hidden * up * sig * (1.0 + gate * (1.0 - sig))).astype(jnp.bfloat16)
    back_up = (back_hidden * gate * sig).astype(jnp.bfloat16)
    back_normed = jnp.dot(back_gate, jnp.transpose(gate_weight), preferred_element_type=jnp.float32)
    back_normed = back_normed + jnp.dot(back_up, jnp.transpose(up_weight), preferred_element_type=jnp.float32)
    scaled = back_normed * norm_gain
    inner = lax.optimization_barrier(jnp.mean(scaled * unit, axis=1, keepdims=True))
    back_latent = scale * (scaled - unit * inner)
    return delta + ASCENT * (target.astype(jnp.float32) + back_latent)
```

```python
import jax
import jax.numpy as jnp
from jax import lax
from jax.experimental import pallas as pl
from jax.experimental.pallas import tpu as pltpu
from jax.sharding import PartitionSpec as P

EPS = 1e-05
ASCENT = 0.5
LAST_SHARE = 0.3
STEP = 512
PAIR = 64
SCOPED_BYTES = 44 << 20

NN = (((1,), (0,)), ((), ()))
NT = (((1,), (1,)), ((), ()))
VMEM = pl.BlockSpec(memory_space=pltpu.VMEM)
HBM = pl.BlockSpec(memory_space=pltpu.HBM)
ANY = pl.BlockSpec(memory_space=pl.ANY)
SMEM = pl.BlockSpec(memory_space=pltpu.SMEM)
F32 = jnp.float32
BF16 = jnp.bfloat16


def dot(a, b, dims):
    return lax.dot_general(a, b, dims, preferred_element_type=F32)


def reversed_bits(value, count):
    out = 0 * value
    bit = 1
    while bit < count:
        out = 2 * out + value // bit % 2
        bit *= 2
    return out


def steps(length):
    return [(at, min(STEP, length - at)) for at in range(0, length, STEP)]


def cost(*products):
    flops = sum(2 * m * k * n for m, k, n in products)
    size = sum(2 * k * n for _, k, n in products)
    return pl.CostEstimate(flops=flops, bytes_accessed=size, transcendentals=0)


def split(x):
    high = x.astype(BF16)
    low = (x - high.astype(F32)).astype(BF16)
    return jnp.concatenate([jnp.broadcast_to(y, (x.shape[0], PAIR)) for y in (high, low)], axis=1)


def joined(x):
    return x[:, :1].astype(F32) + x[:, PAIR : PAIR + 1].astype(F32)


def params():
    return pltpu.CompilerParams(vmem_limit_bytes=SCOPED_BYTES)


def assemble(mirror_ref, blocks, rows_ref, narrow):
    size = blocks[0].shape[0]
    share = len(blocks) // narrow
    for p, block in enumerate(blocks):
        place = (reversed_bits(p // share, narrow) ^ mirror_ref[0]) * share + p % share
        rows_ref[pl.ds(pl.multiple_of(place * size, size), size), :] = block[...]


def forward(mirror, blocks, weights, span, dims, narrow, after, name):
    tokens = sum(b.shape[0] for b in blocks)
    width = blocks[0].shape[1]
    begin, hidden = span
    total = hidden * len(weights)
    half = tokens // 2
    parts = [(i, at, size) for at, size in steps(hidden) for i in range(len(weights))]
    held = (width, hidden) if dims is NN else (hidden, width)

    def cut(ref, at, size):
        return ref.at[:, pl.ds(at, size)] if dims is NN else ref.at[pl.ds(at, size), :]

    def kernel(*refs):
        mirror_ref, refs = refs[0], refs[1:]
        block_refs, refs = refs[: len(blocks)], refs[len(blocks) :]
        weight_refs, refs = refs[: len(weights)], refs[len(weights) + len(after) :]
        keep_ref, send_ref, rows_ref, sems, *held_refs = refs
        copies = [
            pltpu.make_async_copy(cut(weight_refs[i], begin + at, size), cut(held_refs[i], at, size), sems.at[j])
            for j, (i, at, size) in enumerate(parts)
        ]
        for copy in copies:
            copy.start()
        assemble(mirror_ref, block_refs, rows_ref, narrow)
        for copy, (i, at, size) in zip(copies, parts):
            copy.wait()
            part = dot(rows_ref[...], cut(held_refs[i], at, size)[...], dims)
            here = pl.ds(i * hidden + at, size)
            keep_ref[:, here] = part[:half]
            send_ref[:, here] = part[half:].astype(BF16)

    return pl.pallas_call(
        kernel,
        in_specs=[SMEM] + [VMEM] * len(blocks) + [HBM] * len(weights) + [ANY] * len(after),
        out_specs=[VMEM] * 2,
        out_shape=[jax.ShapeDtypeStruct((half, total), F32), jax.ShapeDtypeStruct((half, total), BF16)],
        scratch_shapes=[pltpu.VMEM((tokens, width), BF16), pltpu.SemaphoreType.DMA((len(parts),))]
        + [pltpu.VMEM(held, BF16)] * len(weights),
        compiler_params=params(),
        cost_estimate=cost((tokens, width, total)),
        name=name,
    )(mirror, *blocks, *weights, *after)


def backward(index, blocks, weights, span, before, pieces, name):
    n = len(blocks)
    begin, hidden = span
    share = blocks[0].shape[0]
    tokens = share * n
    width = weights[0].shape[0]
    size = tokens // pieces
    parts = [(i, at, count) for at, count in steps(width) for i in range(len(weights))]
    extra = [] if before is None else [before]

    def kernel(*refs):
        index_ref, refs = refs[0], refs[1:]
        block_refs, refs = refs[:n], refs[n:]
        weight_refs, refs = refs[: len(weights)], refs[len(weights) :]
        before_refs, refs = refs[: len(extra)], refs[len(extra) :]
        out_refs, refs = refs[:pieces], refs[pieces:]
        rows_ref, sems, *held_refs = refs
        copies = [
            pltpu.make_async_copy(
                weight_refs[i].at[pl.ds(at, count), pl.ds(begin, hidden)],
                held_refs[i].at[pl.ds(at, count), :],
                sems.at[j],
            )
            for j, (i, at, count) in enumerate(parts)
        ]
        for copy in copies:
            copy.start()
        for j, block in enumerate(block_refs):
            place = (reversed_bits(j, n) ^ index_ref[0]) * share
            rows_ref[pl.ds(pl.multiple_of(place, share), share), :] = block[...]
        inner = joined(rows_ref[:, pl.ds(2 * hidden, 2 * PAIR)])
        for b in before_refs:
            inner += b[:, pl.ds(width, 1)]
        for i, out in enumerate(out_refs):
            mine = inner[i * size : (i + 1) * size]
            out[:, pl.ds(width, 2 * PAIR)] = split(mine) if i else jnp.broadcast_to(mine, (size, 2 * PAIR))
        for copy, (i, at, count) in zip(copies, parts):
            copy.wait()
            here = pl.ds(at, count)
            product = dot(rows_ref[:, pl.ds(i * hidden, hidden)], held_refs[i][here, :], NT)
            part = part + product if i else product
            if i + 1 == len(weights):
                for b in before_refs:
                    part += b[:, here]
                for j, out in enumerate(out_refs):
                    out[:, here] = part[j * size : (j + 1) * size].astype(out.dtype)

    return pl.pallas_call(
        kernel,
        in_specs=[SMEM] + [VMEM] * n + [HBM] * len(weights) + [VMEM] * len(extra),
        out_specs=[VMEM] * pieces,
        out_shape=[jax.ShapeDtypeStruct((size, width + 2 * PAIR), BF16 if i else F32) for i in range(pieces)],
        scratch_shapes=[
            pltpu.VMEM((tokens, 2 * hidden + 2 * PAIR), BF16),
            pltpu.SemaphoreType.DMA((len(parts),)),
        ]
        + [pltpu.VMEM((width, hidden), BF16)] * len(weights),
        compiler_params=params(),
        cost_estimate=cost((tokens, 2 * hidden, width)),
        name=name,
    )(index, *blocks, *weights, *extra)


def solution(mesh):
    wide, narrow = mesh.shape["wide"], mesh.shape["narrow"]
    share = wide // narrow
    bits = [1 << i for i in range(narrow.bit_length() - 1)]

    def swap(x, axis, k):
        return lax.ppermute(x, axis, [(i, i ^ k) for i in range(mesh.shape[axis])])

    def over_narrow(x):
        return x + sum(swap(x, "narrow", k) for k in range(1, narrow))

    def scatter(keep, send):
        first = None
        for i, bit in enumerate(bits):
            got = swap(send, "narrow", bit)
            first = got if first is None else first
            half = keep.shape[0] // 2
            if i + 1 < len(bits):
                send = (keep[half:] + got[half:].astype(F32)).astype(BF16)
                keep, got = keep[:half], got[:half]
            keep = keep + got.astype(F32)
        return keep, first

    def gather(block):
        blocks = [block]
        for bit in reversed(bits):
            blocks = blocks + [swap(b, "narrow", bit) for b in blocks]
        return blocks

    def gate_terms(sums, back_hidden):
        hidden = sums.shape[1] // 2
        gate, up = sums[:, :hidden], sums[:, hidden:]
        sig = jax.nn.sigmoid(gate)
        back_gate = (back_hidden * up * sig * (1.0 + gate * (1.0 - sig))).astype(BF16)
        back_up = (back_hidden * gate * sig).astype(BF16)
        inner = jnp.sum(back_gate.astype(F32) * gate + back_up.astype(F32) * up, axis=1, keepdims=True)
        return jnp.concatenate([back_gate, back_up, split(inner)], axis=1)

    def on_device(tokens, signs, magnitude, target, norm_gain, gate_weight, up_weight, down_weight):
        width, hidden = gate_weight.shape
        features = width * narrow
        last = max(128, int(hidden * LAST_SHARE) // STEP * STEP)
        span_a, span_b = (0, hidden - last), (hidden - last, last)
        index = lax.axis_index("narrow").astype(jnp.int32).reshape(1)
        mirror = reversed_bits(index, narrow)
        pair = [gate_weight, up_weight]

        targets = [target] + [swap(target, "wide", k) for k in range(1, wide)]
        delta = (2 * signs - 1).astype(F32) * magnitude
        latent = tokens.astype(F32) + delta
        squares = over_narrow(jnp.sum(latent * latent, axis=1, keepdims=True))
        scale = lax.rsqrt(squares / features + EPS)
        unit = latent * scale
        normed = (unit * norm_gain).astype(BF16)
        normeds = [normed] + [swap(normed, "wide", k) for k in range(1, wide)]

        keep, send = forward(mirror, targets, [down_weight], (0, hidden), NT, narrow, [], "back_hidden")
        back_hidden, first = scatter(keep, send)
        keep, send = forward(mirror, normeds, pair, span_a, NN, narrow, [first], "gate_up_a")
        sums_a, first = scatter(keep, send)
        keep, send = forward(mirror, normeds, pair, span_b, NN, narrow, [first], "gate_up_b")
        sums_b, _ = scatter(keep, send)
        blocks_a = gather(gate_terms(sums_a, back_hidden[:, : span_a[1]]))
        blocks_b = gather(gate_terms(sums_b, back_hidden[:, span_b[0] :]))
        (before,) = backward(index, blocks_a, pair, span_a, None, 1, "back_a")
        pieces = backward(index, blocks_b, pair, span_b, before, wide, "back_b")
        back_normed, inner = pieces[0][:, :width], pieces[0][:, width : width + 1]
        for k in range(1, wide):
            got = swap(pieces[k], "wide", k)
            back_normed = back_normed + got[:, :width].astype(F32)
            inner = inner + joined(got[:, width:])
        scaled = back_normed * norm_gain
        back_latent = scale * (scaled - unit * (inner / features))
        return delta + ASCENT * (target.astype(F32) + back_latent)

    rows = P(("groups", "wide"), "narrow")
    in_specs = (rows, rows, rows, rows, P("narrow"), P("narrow", "wide"), P("narrow", "wide"), P("wide", "narrow"))
    return jax.shard_map(on_device, mesh=mesh, in_specs=in_specs, out_specs=rows, check_vma=False)
```

```python
import jax
import jax.numpy as jnp
from jax import lax
from jax.experimental import pallas as pl
from jax.experimental.pallas import tpu as pltpu
from jax.sharding import PartitionSpec as P

EPS = 1e-05
ASCENT = 0.5
LANES = 128
STEP = 512

NN = (((1,), (0,)), ((), ()))
NT = (((1,), (1,)), ((), ()))
ANY = pl.BlockSpec(memory_space=pl.ANY)
HBM = pl.BlockSpec(memory_space=pltpu.HBM)
SMEM = pl.BlockSpec(memory_space=pltpu.SMEM)
VMEM = pl.BlockSpec(memory_space=pltpu.VMEM)
F32 = jnp.float32
BF16 = jnp.bfloat16


def dot(a, b, dims):
    return lax.dot_general(a, b, dims, preferred_element_type=F32)


def steps(length):
    count = next(c for c in range(max(1, length // STEP), length + 1) if length % (c * LANES) == 0)
    return [(i * (length // count), length // count) for i in range(count)]


def params():
    return pltpu.CompilerParams(vmem_limit_bytes=32 << 20)


def in_hbm(weights):
    return [pltpu.with_memory_space_constraint(w, pltpu.HBM) for w in weights]


def cost(m, k, n):
    return pl.CostEstimate(flops=2 * m * k * n, bytes_accessed=2 * k * n, transcendentals=0)


def split(x):
    high = x.astype(BF16)
    low = (x - high.astype(F32)).astype(BF16)
    return jnp.concatenate([jnp.broadcast_to(y, (x.shape[0], LANES // 2)) for y in (high, low)], axis=1)


def joined(x):
    return x[:, :1].astype(F32) + x[:, LANES // 2 : LANES // 2 + 1].astype(F32)


def forward(index, blocks, weights, picks, share, dims, after, name):
    size, width = blocks[0].shape
    tokens = size * len(blocks)
    parts = [(r, i, at, n) for r in range(len(picks)) for at, n in steps(share) for i in range(len(weights))]

    def kernel(index_ref, *refs):
        block_refs, refs = refs[: len(blocks)], refs[len(blocks) :]
        weight_refs, refs = refs[: len(weights)], refs[len(weights) + len(after) :]
        out_ref, rows_ref, held_ref, sems = refs
        copies = []
        for j, (r, i, at, n) in enumerate(parts):
            begin = pl.multiple_of((index_ref[0] ^ picks[r]) * share + at, LANES)
            if dims is NN:
                source, target = weight_refs[i].at[:, pl.ds(begin, n)], held_ref.at[j]
            else:
                source, target = weight_refs[i].at[pl.ds(begin, n), :], held_ref.at[j]
            copies.append(pltpu.make_async_copy(source, target, sems.at[j]))
        for copy in copies:
            copy.start()
        for p, block in enumerate(block_refs):
            rows_ref[p * size : (p + 1) * size, :] = block[...]
        for j, (r, i, at, n) in enumerate(parts):
            copies[j].wait()
            here = pl.ds((r * len(weights) + i) * share + at, n)
            out_ref[:, here] = dot(rows_ref[...], held_ref[j], dims)

    n = parts[0][3]
    total = share * len(picks) * len(weights)
    return pl.pallas_call(
        kernel,
        in_specs=[SMEM] + [VMEM] * len(blocks) + [HBM] * len(weights) + [ANY] * len(after),
        out_specs=VMEM,
        out_shape=jax.ShapeDtypeStruct((tokens, total), F32),
        scratch_shapes=[
            pltpu.VMEM((tokens, width), BF16),
            pltpu.VMEM((len(parts), width, n) if dims is NN else (len(parts), n, width), BF16),
            pltpu.SemaphoreType.DMA((len(parts),)),
        ],
        compiler_params=params(),
        cost_estimate=cost(tokens, width, total),
        name=name,
    )(index, *blocks, *in_hbm(weights), *after)


def backward(index, rows, weights, picks, share, before, pieces, name):
    tokens = rows[0].shape[0]
    width = weights[0].shape[0]
    size = tokens // pieces
    parts = [(r, i, at, n) for at, n in steps(width) for r in range(len(picks)) for i in range(len(weights))]
    extra = [] if before is None else [before]

    def kernel(index_ref, *refs):
        row_refs, refs = refs[: len(picks)], refs[len(picks) :]
        weight_refs, refs = refs[: len(weights)], refs[len(weights) :]
        before_refs, refs = refs[: len(extra)], refs[len(extra) :]
        out_refs, (held_ref, sems) = refs[:pieces], refs[pieces:]
        copies = []
        for j, (r, i, at, n) in enumerate(parts):
            begin = pl.multiple_of((index_ref[0] ^ picks[r]) * share, LANES)
            source = weight_refs[i].at[pl.ds(at, n), pl.ds(begin, share)]
            copies.append(pltpu.make_async_copy(source, held_ref.at[j], sems.at[j]))
        for copy in copies:
            copy.start()
        inner = sum(joined(r[:, pl.ds(2 * share, LANES)]) for r in row_refs)
        for b in before_refs:
            inner += b[:, pl.ds(width, 1)]
        for p, out in enumerate(out_refs):
            mine = inner[p * size : (p + 1) * size]
            out[:, pl.ds(width, LANES)] = split(mine) if p else jnp.broadcast_to(mine, (size, LANES))
        for j, (r, i, at, n) in enumerate(parts):
            copies[j].wait()
            here = pl.ds(at, n)
            product = dot(row_refs[r][:, pl.ds(i * share, share)], held_ref[j], NT)
            part = part + product if r or i else product
            if (r + 1, i + 1) == (len(picks), len(weights)):
                for b in before_refs:
                    part += b[:, here]
                for p, out in enumerate(out_refs):
                    out[:, here] = part[p * size : (p + 1) * size].astype(out.dtype)

    return pl.pallas_call(
        kernel,
        in_specs=[SMEM] + [VMEM] * len(rows) + [HBM] * len(weights) + [VMEM] * len(extra),
        out_specs=[VMEM] * pieces,
        out_shape=[jax.ShapeDtypeStruct((size, width + LANES), BF16 if p else F32) for p in range(pieces)],
        scratch_shapes=[
            pltpu.VMEM((len(parts), parts[0][3], share), BF16),
            pltpu.SemaphoreType.DMA((len(parts),)),
        ],
        compiler_params=params(),
        cost_estimate=cost(tokens, 2 * share * len(picks), width),
        name=name,
    )(index, *rows, *in_hbm(weights), *extra)


def gate_terms(gate, up, back_hidden):
    sig = jax.nn.sigmoid(gate)
    back_gate = (back_hidden * up * sig * (1.0 + gate * (1.0 - sig))).astype(BF16)
    back_up = (back_hidden * gate * sig).astype(BF16)
    return back_gate, back_up


def by_collectives(normed, target, gate_weight, up_weight, down_weight):
    stacked = jnp.stack([normed, target], axis=0)
    rows = lax.all_gather(stacked, "wide", axis=1, tiled=True)
    hidden = gate_weight.shape[1]
    sums = jnp.concatenate(
        [dot(rows[0], gate_weight, NN), dot(rows[0], up_weight, NN), dot(rows[1], down_weight, NT)], axis=1
    )
    sums = lax.psum_scatter(sums, "narrow", scatter_dimension=0, tiled=True)
    both = jnp.concatenate(
        gate_terms(sums[:, :hidden], sums[:, hidden : 2 * hidden], sums[:, 2 * hidden :]), axis=1
    )
    both = lax.all_gather(both, "narrow", axis=0, tiled=True)
    back = dot(both[:, :hidden], gate_weight, NT) + dot(both[:, hidden:], up_weight, NT)
    return lax.psum_scatter(back, "wide", scatter_dimension=0, tiled=True)


def solution(mesh):
    wide, narrow = mesh.shape["wide"], mesh.shape["narrow"]
    near, far = 1, 2

    def swap(x, axis, k):
        return lax.ppermute(x, axis, [(i, i ^ k) for i in range(mesh.shape[axis])])

    def by_swaps(normed, target, gate_weight, up_weight, down_weight):
        width, hidden = gate_weight.shape
        share = hidden // narrow
        index = lax.axis_index("narrow").astype(jnp.int32).reshape(1)
        pair = [gate_weight, up_weight]
        targets = [target] + [swap(target, "wide", k) for k in range(1, wide)]
        normeds = [normed] + [swap(normed, "wide", k) for k in range(1, wide)]

        def hidden_part(picks, after, name):
            return forward(index, targets, [down_weight], picks, share, NT, after, name)

        def pair_part(picks, after, name):
            return forward(index, normeds, pair, picks, share, NN, after, name)

        send = hidden_part([near, near | far], [], "back_hidden_send")
        send, *normeds = lax.optimization_barrier((send, *normeds))
        got = swap(send, "narrow", near)
        keep = hidden_part([0, far], normeds[1:], "back_hidden_keep")
        sum_far = (keep[:, share:] + got[:, share:]).astype(BF16)
        got_far = swap(sum_far, "narrow", far)
        back_hidden = keep[:, :share] + got[:, :share]

        part = pair_part([near | far], [sum_far], "gate_up_near_far")
        part, got_far = lax.optimization_barrier((part, got_far))
        back_hidden = back_hidden + got_far.astype(F32)
        got = swap(part, "narrow", near)
        part = pair_part([far], [part], "gate_up_far")
        sum_far = (part + got).astype(BF16)
        got_far = swap(sum_far, "narrow", far)
        part = pair_part([near, 0], [sum_far], "gate_up_near_own")
        part, got_far = lax.optimization_barrier((part, got_far))
        sums = part[:, 2 * share :] + swap(part[:, : 2 * share], "narrow", near) + got_far.astype(F32)
        gate, up = sums[:, :share], sums[:, share:]
        back_gate, back_up = gate_terms(gate, up, back_hidden)
        inner = jnp.sum(back_gate.astype(F32) * gate + back_up.astype(F32) * up, axis=1, keepdims=True)
        rows = jnp.concatenate([back_gate, back_up, split(inner)], axis=1)

        rows_far = swap(rows, "narrow", far)
        rows_near = swap(rows, "narrow", near)
        (total,) = backward(index, [rows, rows_near], pair, [0, near], share, None, 1, "back_own_near")
        total, rows_far = lax.optimization_barrier((total, rows_far))
        rows_both = swap(rows_far, "narrow", near)
        pieces = backward(
            index, [rows_far, rows_both], pair, [far, near | far], share, total, wide, "back_far_near_far"
        )
        back_normed, inner = pieces[0][:, :width], pieces[0][:, width : width + 1]
        for k in range(1, wide):
            got = swap(pieces[k], "wide", k)
            back_normed = back_normed + got[:, :width].astype(F32)
            inner = inner + joined(got[:, width:])
        return back_normed, inner

    def on_device(tokens, signs, magnitude, target, norm_gain, gate_weight, up_weight, down_weight):
        width, hidden = gate_weight.shape
        features = width * narrow
        weights = (gate_weight, up_weight, down_weight)
        square = narrow == (near | far) + 1 and hidden % (narrow * LANES) == 0 and wide & (wide - 1) == 0

        delta = (2 * signs - 1).astype(F32) * magnitude
        latent = tokens.astype(F32) + delta
        squares = jnp.sum(latent * latent, axis=1, keepdims=True)
        if square:
            squares = squares + sum(swap(squares, "narrow", k) for k in range(1, narrow))
        else:
            squares = lax.psum(squares, "narrow")
        scale = lax.rsqrt(squares / features + EPS)
        unit = latent * scale
        normed = (unit * norm_gain).astype(BF16)
        if square:
            back_normed, inner = by_swaps(normed, target, *weights)
            scaled = back_normed * norm_gain
        else:
            scaled = by_collectives(normed, target, *weights) * norm_gain
            inner = lax.psum(jnp.sum(scaled * unit, axis=1, keepdims=True), "narrow")
        back_latent = scale * (scaled - unit * (inner / features))
        return delta + ASCENT * (target.astype(F32) + back_latent)

    rows = P(("groups", "wide"), "narrow")
    in_specs = (rows, rows, rows, rows, P("narrow"), P("narrow", "wide"), P("narrow", "wide"), P("wide", "narrow"))
    return jax.shard_map(on_device, mesh=mesh, in_specs=in_specs, out_specs=rows, check_vma=False)
```

```python
import jax
import jax.numpy as jnp
from jax import lax
from jax.experimental import pallas as pl
from jax.experimental.pallas import tpu as pltpu
from jax.sharding import PartitionSpec as P

EPS = 1e-05
ASCENT = 0.5
LANES = 128
STEP = 512
FIRST_FLYING = 8

NN = (((1,), (0,)), ((), ()))
NT = (((1,), (1,)), ((), ()))
ANY = pl.BlockSpec(memory_space=pl.ANY)
HBM = pl.BlockSpec(memory_space=pltpu.HBM)
SMEM = pl.BlockSpec(memory_space=pltpu.SMEM)
VMEM = pl.BlockSpec(memory_space=pltpu.VMEM)
F32 = jnp.float32
BF16 = jnp.bfloat16


def dot(a, b, dims):
    return lax.dot_general(a, b, dims, preferred_element_type=F32)


def steps(length):
    count = next(c for c in range(max(1, length // STEP), length + 1) if length % (c * LANES) == 0)
    return [(i * (length // count), length // count) for i in range(count)]


def params(mebibytes):
    return pltpu.CompilerParams(vmem_limit_bytes=mebibytes << 20)


def in_hbm(arrays):
    return [pltpu.with_memory_space_constraint(x, pltpu.HBM) for x in arrays]


def in_vmem(x):
    return pltpu.with_memory_space_constraint(x, pltpu.VMEM)


def cost(m, k, n):
    return pl.CostEstimate(flops=2 * m * k * n, bytes_accessed=2 * k * n, transcendentals=0)


def split(x):
    high = x.astype(BF16)
    low = (x - high.astype(F32)).astype(BF16)
    return jnp.concatenate([jnp.broadcast_to(y, (x.shape[0], LANES // 2)) for y in (high, low)], axis=1)


def joined(x):
    return x[:, :1].astype(F32) + x[:, LANES // 2 : LANES // 2 + 1].astype(F32)


def bring(index_ref, pick, share, sources, target_ref, place, sems, first=0):
    copies = []
    for at, n in steps(share):
        for i, source in enumerate(sources):
            begin = pl.multiple_of((index_ref[0] ^ pick) * share + at, LANES)
            copies.append(
                pltpu.make_async_copy(
                    source.at[:, pl.ds(begin, n)],
                    target_ref.at[place + i, :, pl.ds(at, n)],
                    sems.at[first + len(copies)],
                )
            )
    return copies


def hidden_gradient(index, blocks, down_weight, pair, pick, picks, share):
    size, width = blocks[0].shape
    tokens = size * len(blocks)
    parts = [(r, at, n) for r in range(len(picks)) for at, n in steps(share)]
    half = len(picks) // 2

    def kernel(index_ref, *refs):
        block_refs, refs = refs[: len(blocks)], refs[len(blocks) :]
        down_ref, refs = refs[0], refs[1:]
        pair_refs, refs = refs[: len(pair)], refs[len(pair) :]
        out_refs, refs = refs[:2], refs[2:]
        held_ref, rows_ref, down_parts, sems, pair_sems = refs
        copies = []
        for j, (r, at, n) in enumerate(parts):
            begin = pl.multiple_of((index_ref[0] ^ picks[r]) * share + at, LANES)
            copies.append(pltpu.make_async_copy(down_ref.at[pl.ds(begin, n), :], down_parts.at[j], sems.at[j]))
        copies += bring(index_ref, pick, share, pair_refs, held_ref, 0, pair_sems)
        for copy in copies[:FIRST_FLYING]:
            copy.start()
        for p, block in enumerate(block_refs):
            rows_ref[p * size : (p + 1) * size, :] = block[...]
        for j, (r, at, n) in enumerate(parts):
            copies[j].wait()
            for copy in copies[j + FIRST_FLYING : j + FIRST_FLYING + 1]:
                copy.start()
            out_refs[r // half][:, pl.ds(r % half * share + at, n)] = dot(rows_ref[...], down_parts[j], NT)
        for copy in copies[len(parts) + FIRST_FLYING :]:
            copy.start()
        for copy in copies[len(parts) :]:
            copy.wait()

    count = len(steps(share))
    total = len(picks) * share
    return pl.pallas_call(
        kernel,
        in_specs=[SMEM] + [VMEM] * len(blocks) + [HBM] * (1 + len(pair)),
        out_specs=[VMEM] * 3,
        out_shape=[jax.ShapeDtypeStruct((tokens, half * share), F32)] * 2
        + [pltpu.VMEM((len(pair), width, share), BF16)],
        scratch_shapes=[
            pltpu.VMEM((tokens, width), BF16),
            pltpu.VMEM((len(parts), parts[0][2], width), BF16),
            pltpu.SemaphoreType.DMA((len(parts),)),
            pltpu.SemaphoreType.DMA((len(pair) * count,)),
        ],
        compiler_params=params(26),
        cost_estimate=cost(tokens, width, total),
        name="back_hidden",
    )(index, *blocks, *in_hbm([down_weight, *pair]))


def gate_and_up(index, blocks, held, pair, picks, both, after, name):
    size, width = blocks[0].shape
    tokens = size * len(blocks)
    share = held.shape[2]
    outs = 2 if both else 1
    count = len(steps(share)) * len(pair)

    def kernel(index_ref, *refs):
        block_refs, refs = refs[: len(blocks)], refs[len(blocks) :]
        held_ref, refs = refs[0], refs[1:]
        pair_refs, refs = refs[: len(pair)], refs[len(pair) + len(after) :]
        out_refs, (next_ref, rows_ref, sems) = refs[:outs], refs[outs:]
        copies = []
        for k, pick in enumerate(picks):
            copies += bring(index_ref, pick, share, pair_refs, next_ref, k * len(pair), sems, k * count)
        for copy in copies:
            copy.start()
        for p, block in enumerate(block_refs):
            rows_ref[p * size : (p + 1) * size, :] = block[...]
        n = steps(share)[0][1]

        @pl.loop(0, share // n)
        def _(step):
            for i in range(len(pair)):
                part = dot(rows_ref[...], held_ref[i, :, pl.ds(pl.multiple_of(step * n, n), n)], NN)
                out_refs[0][:, pl.ds(pl.multiple_of(i * share + step * n, LANES), n)] = part

        for j, copy in enumerate(copies):
            copy.wait()
            if both and j < count:
                at, n = steps(share)[j // len(pair)]
                i = j % len(pair)
                part = dot(rows_ref[...], next_ref[i, :, pl.ds(at, n)], NN)
                out_refs[1][:, pl.ds(i * share + at, n)] = part

    return pl.pallas_call(
        kernel,
        in_specs=[SMEM] + [VMEM] * (len(blocks) + 1) + [HBM] * len(pair) + [ANY] * len(after),
        out_specs=[VMEM] * (outs + 1),
        out_shape=[jax.ShapeDtypeStruct((tokens, len(pair) * share), F32)] * outs
        + [pltpu.VMEM((len(pair) * len(picks), width, share), BF16)],
        scratch_shapes=[pltpu.VMEM((tokens, width), BF16), pltpu.SemaphoreType.DMA((count * len(picks),))],
        compiler_params=params(8),
        cost_estimate=cost(tokens, width, outs * len(pair) * share),
        name=name,
    )(index, *blocks, in_vmem(held), *in_hbm(pair), *after)


def backward(index, rows, held, pair, pick, stays, before, pieces, name):
    tokens = rows[0].shape[0]
    _, width, share = held.shape
    size = tokens // pieces
    extra = [] if before is None else [before]
    n = steps(width)[0][1]
    now = held.shape[0] // len(pair)

    def kernel(index_ref, *refs):
        row_refs, refs = refs[: len(rows)], refs[len(rows) :]
        held_ref, refs = refs[0], refs[1:]
        before_refs, refs = refs[: len(extra)], refs[len(extra) :]
        pair_refs, refs = refs[: len(pair)], refs[len(pair) :]
        out_refs, (next_ref, *sums_ref, sems) = refs[:pieces], refs[pieces:]
        copies = bring(index_ref, pick, share, pair_refs, next_ref, 0, sems)
        for copy in copies:
            copy.start()
        inner = sum(joined(r[:, pl.ds(2 * share, LANES)]) for r in row_refs)
        for b in before_refs:
            inner += b[:, pl.ds(width, 1)]
        for p, out in enumerate(out_refs):
            mine = inner[p * size : (p + 1) * size]
            out[:, pl.ds(width, LANES)] = split(mine) if p else jnp.broadcast_to(mine, (size, LANES))

        def products(weights, those, here):
            pairs = [(row, i) for row in range(len(those)) for i in range(len(pair))]
            return sum(
                dot(those[row][:, pl.ds(i * share, share)], weights[row * len(pair) + i, here, :], NT)
                for row, i in pairs
            )

        def finish(part, here):
            for b in before_refs:
                part += b[:, here]
            for p, out in enumerate(out_refs):
                out[:, here] = part[p * size : (p + 1) * size].astype(out.dtype)

        @pl.loop(0, width // n)
        def _(step):
            here = pl.ds(pl.multiple_of(step * n, n), n)
            part = products(held_ref, row_refs[:now], here)
            if stays:
                finish(part, here)
            else:
                sums_ref[0][:, here] = part

        for copy in copies:
            copy.wait()
        if not stays:

            @pl.loop(0, width // n)
            def _(step):
                here = pl.ds(pl.multiple_of(step * n, n), n)
                finish(sums_ref[0][:, here] + products(next_ref, row_refs[now:], here), here)

    brought = pltpu.VMEM((len(pair), width, share), BF16)
    return pl.pallas_call(
        kernel,
        in_specs=[SMEM] + [VMEM] * (len(rows) + 1 + len(extra)) + [HBM] * len(pair),
        out_specs=[VMEM] * (pieces + stays),
        out_shape=[jax.ShapeDtypeStruct((size, width + LANES), BF16 if p else F32) for p in range(pieces)]
        + [brought] * stays,
        scratch_shapes=([] if stays else [brought, pltpu.VMEM((tokens, width), F32)])
        + [pltpu.SemaphoreType.DMA((len(steps(share)) * len(pair),))],
        compiler_params=params(8 if stays else 16),
        cost_estimate=cost(tokens, len(pair) * len(rows) * share, width),
        name=name,
    )(index, *rows, in_vmem(held), *extra, *in_hbm(pair))


def latents(tokens, signs, magnitude, gain, target):
    given = (tokens, signs, magnitude)

    def kernel(*refs):
        sources, (delta_ref, latent_ref, squares_ref, *same_refs), scratch = refs[:5], refs[5:10], refs[10:]
        copies = [
            pltpu.make_async_copy(source, target, scratch[-1].at[i])
            for i, (source, target) in enumerate(zip(sources, (*scratch[:-1], *same_refs)))
        ]
        for copy in copies:
            copy.start()
        for copy in copies[: len(given)]:
            copy.wait()
        delta = (2 * scratch[1][...] - 1).astype(F32) * scratch[2][...]
        latent = scratch[0][...].astype(F32) + delta
        delta_ref[...] = delta
        latent_ref[...] = latent
        squares_ref[...] = jnp.sum(latent * latent, axis=1, keepdims=True)
        for copy in copies[len(given) :]:
            copy.wait()

    whole = jax.ShapeDtypeStruct(tokens.shape, F32)
    return pl.pallas_call(
        kernel,
        in_specs=[HBM] * 5,
        out_specs=[VMEM] * 5,
        out_shape=[
            whole,
            whole,
            jax.ShapeDtypeStruct((tokens.shape[0], 1), F32),
            jax.ShapeDtypeStruct(gain.shape, F32),
            jax.ShapeDtypeStruct(target.shape, target.dtype),
        ],
        scratch_shapes=[pltpu.VMEM(x.shape, x.dtype) for x in given] + [pltpu.SemaphoreType.DMA((5,))],
        compiler_params=params(8),
        cost_estimate=pl.CostEstimate(flops=8 * tokens.size, bytes_accessed=18 * tokens.size, transcendentals=0),
        name="latents",
    )(*in_hbm([*given, gain, target]))


def gate_terms(gate, up, back_hidden):
    sig = jax.nn.sigmoid(gate)
    back_gate = (back_hidden * up * sig * (1.0 + gate * (1.0 - sig))).astype(BF16)
    back_up = (back_hidden * gate * sig).astype(BF16)
    return back_gate, back_up


def gate_rows(own, got_near, got_far, hidden_own, hidden_near, hidden_far, held):
    tokens, share = hidden_far.shape

    def kernel(own_ref, near_ref, far_ref, hidden_own_ref, hidden_near_ref, hidden_far_ref, _, rows_ref, __):
        inner = jnp.zeros((tokens, 1), F32)
        for at, n in steps(share):
            here, there = pl.ds(at, n), pl.ds(share + at, n)
            gate, up = (own_ref[:, x] + near_ref[:, x] + far_ref[:, x].astype(F32) for x in (here, there))
            back_hidden = hidden_own_ref[:, here] + hidden_near_ref[:, here] + hidden_far_ref[:, here].astype(F32)
            back_gate, back_up = gate_terms(gate, up, back_hidden)
            rows_ref[:, here] = back_gate
            rows_ref[:, there] = back_up
            products = back_gate.astype(F32) * gate + back_up.astype(F32) * up
            inner += jnp.sum(products, axis=1, keepdims=True)
        rows_ref[:, pl.ds(2 * share, LANES)] = split(inner)

    return pl.pallas_call(
        kernel,
        in_specs=[VMEM] * 7,
        out_specs=[VMEM] * 2,
        out_shape=[
            jax.ShapeDtypeStruct((tokens, 2 * share + LANES), BF16),
            pltpu.VMEM(held.shape, held.dtype),
        ],
        input_output_aliases={6: 1},
        compiler_params=params(8),
        cost_estimate=pl.CostEstimate(
            flops=20 * tokens * share, bytes_accessed=30 * tokens * share, transcendentals=tokens * share
        ),
        name="gate",
    )(own, got_near, got_far, hidden_own, hidden_near, hidden_far, in_vmem(held))


def by_collectives(normed, target, gate_weight, up_weight, down_weight):
    stacked = jnp.stack([normed, target], axis=0)
    rows = lax.all_gather(stacked, "wide", axis=1, tiled=True)
    hidden = gate_weight.shape[1]
    sums = jnp.concatenate(
        [dot(rows[0], gate_weight, NN), dot(rows[0], up_weight, NN), dot(rows[1], down_weight, NT)], axis=1
    )
    sums = lax.psum_scatter(sums, "narrow", scatter_dimension=0, tiled=True)
    both = jnp.concatenate(
        gate_terms(sums[:, :hidden], sums[:, hidden : 2 * hidden], sums[:, 2 * hidden :]), axis=1
    )
    both = lax.all_gather(both, "narrow", axis=0, tiled=True)
    back = dot(both[:, :hidden], gate_weight, NT) + dot(both[:, hidden:], up_weight, NT)
    return lax.psum_scatter(back, "wide", scatter_dimension=0, tiled=True)


def solution(mesh):
    wide, narrow = mesh.shape["wide"], mesh.shape["narrow"]
    near, far = 1, 2

    def swap(x, axis, k):
        return lax.ppermute(x, axis, [(i, i ^ k) for i in range(mesh.shape[axis])])

    def by_swaps(normed, target, own_target, gate_weight, up_weight, down_weight):
        width, hidden = gate_weight.shape
        share = hidden // narrow
        index = lax.axis_index("narrow").astype(jnp.int32).reshape(1)
        pair = [gate_weight, up_weight]
        diagonal = near | far
        targets = [own_target] + [swap(target, "wide", k) for k in range(1, wide)]
        normeds = [normed] + [swap(normed, "wide", k) for k in range(1, wide)]

        send, keep, held_diagonal = hidden_gradient(
            index, targets, down_weight, pair, diagonal, [near, diagonal, 0, far], share
        )
        send, *normeds = lax.optimization_barrier((send, *normeds))
        got = swap(send, "narrow", near)
        part, held_far = gate_and_up(
            index, normeds, held_diagonal, pair, [far], False, [send], "gate_up_diagonal"
        )
        part, got = lax.optimization_barrier((part, got))
        hidden_far = swap((keep[:, share:] + got[:, share:]).astype(BF16), "narrow", far)
        hidden_near = got
        got = swap(part, "narrow", near)
        part, held_near = gate_and_up(index, normeds, held_far, pair, [near], False, [part], "gate_up_far")
        part, got, hidden_far = lax.optimization_barrier((part, got, hidden_far))
        sum_far = (part + got).astype(BF16)
        got_far = swap(sum_far, "narrow", far)
        part, own, held = gate_and_up(
            index, normeds, held_near, pair, [0, near], True, [sum_far], "gate_up_near_own"
        )
        part, got_far = lax.optimization_barrier((part, got_far))
        got = swap(part, "narrow", near)
        rows, held = gate_rows(own, got, got_far, keep, hidden_near, hidden_far, held)

        rows_far = swap(rows, "narrow", far)
        rows_near = swap(rows, "narrow", near)
        total, held = backward(
            index, [rows, rows_near], held, pair, far, True, None, 1, "back_own_near"
        )
        total, rows_far = lax.optimization_barrier((total, rows_far))
        rows_diagonal = swap(rows_far, "narrow", near)
        pieces = backward(
            index, [rows_far, rows_diagonal], held, pair, diagonal, False, total, wide, "back_far_diagonal"
        )
        back_normed, inner = pieces[0][:, :width], pieces[0][:, width : width + 1]
        for k in range(1, wide):
            got = swap(pieces[k], "wide", k)
            back_normed = back_normed + got[:, :width].astype(F32)
            inner = inner + joined(got[:, width:])
        return back_normed, inner

    def on_device(tokens, signs, magnitude, target, norm_gain, gate_weight, up_weight, down_weight):
        width, hidden = gate_weight.shape
        features = width * narrow
        weights = (gate_weight, up_weight, down_weight)
        square = narrow == (near | far) + 1 and hidden % (narrow * LANES) == 0 and wide & (wide - 1) == 0

        delta, latent, squares, gain, own_target = latents(
            tokens, signs, magnitude, norm_gain.reshape(1, -1), target
        )
        if square:
            squares = squares + sum(swap(squares, "narrow", k) for k in range(1, narrow))
        else:
            squares = lax.psum(squares, "narrow")
        scale = lax.rsqrt(squares / features + EPS)
        unit = latent * scale
        normed = (unit * gain).astype(BF16)
        if square:
            back_normed, inner = by_swaps(normed, target, own_target, *weights)
            scaled = back_normed * gain
        else:
            scaled = by_collectives(normed, target, *weights) * gain
            inner = lax.psum(jnp.sum(scaled * unit, axis=1, keepdims=True), "narrow")
        back_latent = scale * (scaled - unit * (inner / features))
        return delta + ASCENT * (own_target.astype(F32) + back_latent)

    rows = P(("groups", "wide"), "narrow")
    in_specs = (rows, rows, rows, rows, P("narrow"), P("narrow", "wide"), P("narrow", "wide"), P("wide", "narrow"))
    return jax.shard_map(on_device, mesh=mesh, in_specs=in_specs, out_specs=rows, check_vma=False)
```

```python
import jax
import jax.numpy as jnp
from jax import lax
from jax.experimental import pallas as pl
from jax.experimental.pallas import tpu as pltpu
from jax.sharding import PartitionSpec as P

EPS = 1e-05
ASCENT = 0.5
LANES = 128
STEP = 512

NN = (((1,), (0,)), ((), ()))
NT = (((1,), (1,)), ((), ()))
ANY = pl.BlockSpec(memory_space=pl.ANY)
HBM = pl.BlockSpec(memory_space=pltpu.HBM)
SMEM = pl.BlockSpec(memory_space=pltpu.SMEM)
VMEM = pl.BlockSpec(memory_space=pltpu.VMEM)
F32 = jnp.float32
BF16 = jnp.bfloat16


def dot(a, b, dims):
    return lax.dot_general(a, b, dims, preferred_element_type=F32)


def steps(length):
    count = next(c for c in range(max(1, length // STEP), length + 1) if length % (c * LANES) == 0)
    return [(i * (length // count), length // count) for i in range(count)]


def params(mebibytes):
    return pltpu.CompilerParams(vmem_limit_bytes=mebibytes << 20)


def in_hbm(arrays):
    return [pltpu.with_memory_space_constraint(x, pltpu.HBM) for x in arrays]


def in_vmem(x):
    return pltpu.with_memory_space_constraint(x, pltpu.VMEM)


def cost(m, k, n):
    return pl.CostEstimate(flops=2 * m * k * n, bytes_accessed=2 * k * n, transcendentals=0)


def split(x):
    high = x.astype(BF16)
    low = (x - high.astype(F32)).astype(BF16)
    return jnp.concatenate([jnp.broadcast_to(y, (x.shape[0], LANES // 2)) for y in (high, low)], axis=1)


def joined(x):
    return x[:, :1].astype(F32) + x[:, LANES // 2 : LANES // 2 + 1].astype(F32)


def bring(index_ref, pick, share, sources, target_ref, place, sems, first=0):
    copies = []
    for at, n in steps(share):
        for i, source in enumerate(sources):
            begin = pl.multiple_of((index_ref[0] ^ pick) * share + at, LANES)
            copies.append(
                pltpu.make_async_copy(
                    source.at[:, pl.ds(begin, n)],
                    target_ref.at[place + i, :, pl.ds(at, n)],
                    sems.at[first + len(copies)],
                )
            )
    return copies


def rows_ahead(index, down_weight, picks, share):
    width = down_weight.shape[1]

    def kernel(index_ref, down_ref, out_ref, sems):
        copies = []
        for r, pick in enumerate(picks):
            begin = pl.multiple_of((index_ref[0] ^ pick) * share, LANES)
            source, target = down_ref.at[pl.ds(begin, share), :], out_ref.at[pl.ds(r * share, share), :]
            copies.append(pltpu.make_async_copy(source, target, sems.at[r]))
        for copy in copies:
            copy.start()
        for copy in copies:
            copy.wait()

    return pl.pallas_call(
        kernel,
        in_specs=[SMEM, HBM],
        out_specs=VMEM,
        out_shape=pltpu.VMEM((len(picks) * share, width), down_weight.dtype),
        scratch_shapes=[pltpu.SemaphoreType.DMA((len(picks),))],
        compiler_params=params(8),
        cost_estimate=cost(8, width, len(picks) * share),
        name="rows_ahead",
    )(index, *in_hbm([down_weight]))


def hidden_gradient(index, blocks, held, down_weight, pair, pick, picks, share):
    size, width = blocks[0].shape
    tokens = size * len(blocks)
    first = held.shape[0] // share
    parts = [(r, at, n) for r in range(first, len(picks)) for at, n in steps(share)]
    n = parts[0][2]
    half = len(picks) // 2 * share

    def kernel(index_ref, *refs):
        block_refs, refs = refs[: len(blocks)], refs[len(blocks) :]
        held_ref, down_ref, refs = refs[0], refs[1], refs[2:]
        pair_refs, refs = refs[: len(pair)], refs[len(pair) :]
        send_ref, keep_ref, next_ref, rows_ref, down_parts, sems, pair_sems = refs
        copies = []
        for j, (r, at, _) in enumerate(parts):
            begin = pl.multiple_of((index_ref[0] ^ picks[r]) * share + at, LANES)
            copies.append(pltpu.make_async_copy(down_ref.at[pl.ds(begin, n), :], down_parts.at[j], sems.at[j]))
        later = bring(index_ref, pick, share, pair_refs, next_ref, 0, pair_sems)
        for copy in copies + later:
            copy.start()
        for p, block in enumerate(block_refs):
            rows_ref[p * size : (p + 1) * size, :] = block[...]

        @pl.loop(0, held.shape[0] // n)
        def _(step):
            here = pl.ds(pl.multiple_of(step * n, n), n)
            send_ref[:, here] = dot(rows_ref[...], held_ref[here, :], NT).astype(BF16)

        for j, (r, at, _) in enumerate(parts):
            copies[j].wait()
            here, part = r * share + at, dot(rows_ref[...], down_parts[j], NT)
            if here < half:
                send_ref[:, pl.ds(here, n)] = part.astype(BF16)
            else:
                keep_ref[:, pl.ds(here - half, n)] = part
        for copy in later:
            copy.wait()

    count = len(steps(share))
    return pl.pallas_call(
        kernel,
        in_specs=[SMEM] + [VMEM] * (len(blocks) + 1) + [HBM] * (1 + len(pair)),
        out_specs=[VMEM] * 3,
        out_shape=[
            jax.ShapeDtypeStruct((tokens, half), BF16),
            jax.ShapeDtypeStruct((tokens, half), F32),
            pltpu.VMEM((len(pair), width, share), BF16),
        ],
        scratch_shapes=[
            pltpu.VMEM((tokens, width), BF16),
            pltpu.VMEM((len(parts), n, width), BF16),
            pltpu.SemaphoreType.DMA((len(parts),)),
            pltpu.SemaphoreType.DMA((len(pair) * count,)),
        ],
        compiler_params=params(22),
        cost_estimate=cost(tokens, width, len(picks) * share),
        name="back_hidden",
    )(index, *blocks, in_vmem(held), *in_hbm([down_weight, *pair]))


def gate_and_up(index, blocks, held, pair, picks, share, after, name, stays=True):
    size, width = blocks[0].shape
    tokens = size * len(blocks)
    given = [] if held is None else [held]
    use = held is None
    outs = len(picks) if use else 1
    count = len(steps(share)) * len(pair)

    def kernel(index_ref, *refs):
        block_refs, refs = refs[: len(blocks)], refs[len(blocks) :]
        held_refs, refs = refs[: len(given)], refs[len(given) :]
        pair_refs, refs = refs[: len(pair)], refs[len(pair) + len(after) :]
        out_refs, (*next_ref, rows_ref, sems) = refs[:outs], refs[outs:]
        copies = []
        for k, pick in enumerate(picks):
            copies += bring(index_ref, pick, share, pair_refs, next_ref[0], k * len(pair), sems, k * count)
        for copy in copies:
            copy.start()
        for p, block in enumerate(block_refs):
            rows_ref[p * size : (p + 1) * size, :] = block[...]
        n = steps(share)[0][1]
        for held_ref, out in zip(held_refs, out_refs):

            @pl.loop(0, share // n)
            def _(step):
                for i in range(len(pair)):
                    part = dot(rows_ref[...], held_ref[i, :, pl.ds(pl.multiple_of(step * n, n), n)], NN)
                    out[:, pl.ds(pl.multiple_of(i * share + step * n, LANES), n)] = part

        for j, copy in enumerate(copies):
            copy.wait()
            if use:
                k, (at, n), i = j // count, steps(share)[j % count // len(pair)], j % len(pair)
                part = dot(rows_ref[...], next_ref[0][k * len(pair) + i, :, pl.ds(at, n)], NN)
                out_refs[k][:, pl.ds(i * share + at, n)] = part.astype(out_refs[k].dtype)

    brought = [pltpu.VMEM((len(pair) * len(picks), width, share), BF16)] if picks else []
    more, scratch = (brought, []) if stays else ([], brought)
    return pl.pallas_call(
        kernel,
        in_specs=[SMEM] + [VMEM] * (len(blocks) + len(given)) + [HBM] * len(pair) + [ANY] * len(after),
        out_specs=[VMEM] * (outs + len(more)),
        out_shape=[jax.ShapeDtypeStruct((tokens, len(pair) * share), BF16 if i else F32) for i in range(outs)] + more,
        scratch_shapes=scratch
        + [
            pltpu.VMEM((tokens, width), BF16),
            pltpu.SemaphoreType.DMA((max(1, count * len(picks)),)),
        ],
        compiler_params=params(8 if stays else 20),
        cost_estimate=cost(tokens, width, outs * len(pair) * share),
        name=name,
    )(index, *blocks, *[in_vmem(h) for h in given], *in_hbm(pair), *after)


def backward(index, rows, held, pair, picks, before, pieces, name):
    tokens = rows[0].shape[0]
    _, width, share = held.shape
    size = tokens // pieces
    extra = [] if before is None else [before]
    count = len(steps(share)) * len(pair)
    n = steps(width)[0][1]

    def kernel(index_ref, *refs):
        row_refs, refs = refs[: len(rows)], refs[len(rows) :]
        held_ref, refs = refs[0], refs[1:]
        before_refs, refs = refs[: len(extra)], refs[len(extra) :]
        pair_refs, refs = refs[: len(pair)], refs[len(pair) :]
        out_refs, refs = refs[:pieces], refs[pieces:]
        copies = []
        for k, pick in enumerate(picks):
            copies += bring(index_ref, pick, share, pair_refs, refs[0], k * len(pair), refs[1], k * count)
        for copy in copies:
            copy.start()
        inner = sum(joined(r[:, pl.ds(2 * share, LANES)]) for r in row_refs)
        for b in before_refs:
            inner += b[:, pl.ds(width, 1)]
        for p, out in enumerate(out_refs):
            mine = inner[p * size : (p + 1) * size]
            out[:, pl.ds(width, LANES)] = split(mine) if p else jnp.broadcast_to(mine, (size, LANES))

        @pl.loop(0, width // n)
        def _(step):
            here = pl.ds(pl.multiple_of(step * n, n), n)
            part = sum(
                dot(row_refs[j // 2][:, pl.ds(j % 2 * share, share)], held_ref[j, here, :], NT)
                for j in range(2 * len(rows))
            )
            for b in before_refs:
                part += b[:, here]
            for p, out in enumerate(out_refs):
                out[:, here] = part[p * size : (p + 1) * size].astype(out.dtype)

        for copy in copies:
            copy.wait()

    more = [pltpu.VMEM((len(pair) * len(picks), width, share), BF16)] if picks else []
    return pl.pallas_call(
        kernel,
        in_specs=[SMEM] + [VMEM] * (len(rows) + 1 + len(extra)) + [HBM] * len(pair),
        out_specs=[VMEM] * (pieces + len(more)),
        out_shape=[jax.ShapeDtypeStruct((size, width + LANES), BF16 if p else F32) for p in range(pieces)] + more,
        scratch_shapes=[pltpu.SemaphoreType.DMA((max(1, count * len(picks)),))],
        compiler_params=params(8),
        cost_estimate=cost(tokens, held.shape[0] * share, width),
        name=name,
    )(index, *rows, in_vmem(held), *extra, *in_hbm(pair))


def latents(tokens, signs, magnitude, gain, target):
    given = (tokens, signs, magnitude)

    def kernel(*refs):
        sources, (delta_ref, latent_ref, squares_ref, *same_refs), scratch = refs[:5], refs[5:10], refs[10:]
        copies = [
            pltpu.make_async_copy(source, target, scratch[-1].at[i])
            for i, (source, target) in enumerate(zip(sources, (*scratch[:-1], *same_refs)))
        ]
        for copy in copies:
            copy.start()
        for copy in copies[: len(given)]:
            copy.wait()
        delta = (2 * scratch[1][...] - 1).astype(F32) * scratch[2][...]
        latent = scratch[0][...].astype(F32) + delta
        delta_ref[...] = delta
        latent_ref[...] = latent
        squares_ref[...] = jnp.sum(latent * latent, axis=1, keepdims=True)
        for copy in copies[len(given) :]:
            copy.wait()

    whole = jax.ShapeDtypeStruct(tokens.shape, F32)
    return pl.pallas_call(
        kernel,
        in_specs=[HBM] * 5,
        out_specs=[VMEM] * 5,
        out_shape=[
            whole,
            whole,
            jax.ShapeDtypeStruct((tokens.shape[0], 1), F32),
            jax.ShapeDtypeStruct(gain.shape, F32),
            jax.ShapeDtypeStruct(target.shape, target.dtype),
        ],
        scratch_shapes=[pltpu.VMEM(x.shape, x.dtype) for x in given] + [pltpu.SemaphoreType.DMA((5,))],
        compiler_params=params(8),
        cost_estimate=pl.CostEstimate(flops=8 * tokens.size, bytes_accessed=18 * tokens.size, transcendentals=0),
        name="latents",
    )(*in_hbm([*given, gain, target]))


def gate_terms(gate, up, back_hidden):
    sig = jax.nn.sigmoid(gate)
    back_gate = (back_hidden * up * sig * (1.0 + gate * (1.0 - sig))).astype(BF16)
    back_up = (back_hidden * gate * sig).astype(BF16)
    return back_gate, back_up


def gate_rows(own, got_near, got_far, hidden_own, hidden_near, hidden_far, held):
    tokens, share = hidden_far.shape

    def kernel(own_ref, near_ref, far_ref, hidden_own_ref, hidden_near_ref, hidden_far_ref, _, rows_ref, __):
        inner = jnp.zeros((tokens, 1), F32)
        for at, n in steps(share):
            here, there = pl.ds(at, n), pl.ds(share + at, n)
            gate, up = (
                own_ref[:, x] + near_ref[:, x].astype(F32) + far_ref[:, x].astype(F32) for x in (here, there)
            )
            back_hidden = hidden_own_ref[:, here] + hidden_near_ref[:, here].astype(F32)
            back_hidden += hidden_far_ref[:, here].astype(F32)
            back_gate, back_up = gate_terms(gate, up, back_hidden)
            rows_ref[:, here] = back_gate
            rows_ref[:, there] = back_up
            products = back_gate.astype(F32) * gate + back_up.astype(F32) * up
            inner += jnp.sum(products, axis=1, keepdims=True)
        rows_ref[:, pl.ds(2 * share, LANES)] = split(inner)

    return pl.pallas_call(
        kernel,
        in_specs=[VMEM] * 7,
        out_specs=[VMEM] * 2,
        out_shape=[
            jax.ShapeDtypeStruct((tokens, 2 * share + LANES), BF16),
            pltpu.VMEM(held.shape, held.dtype),
        ],
        input_output_aliases={6: 1},
        compiler_params=params(8),
        cost_estimate=pl.CostEstimate(
            flops=20 * tokens * share, bytes_accessed=30 * tokens * share, transcendentals=tokens * share
        ),
        name="gate",
    )(own, got_near, got_far, hidden_own, hidden_near, hidden_far, in_vmem(held))


def by_collectives(normed, target, gate_weight, up_weight, down_weight):
    stacked = jnp.stack([normed, target], axis=0)
    rows = lax.all_gather(stacked, "wide", axis=1, tiled=True)
    hidden = gate_weight.shape[1]
    sums = jnp.concatenate(
        [dot(rows[0], gate_weight, NN), dot(rows[0], up_weight, NN), dot(rows[1], down_weight, NT)], axis=1
    )
    sums = lax.psum_scatter(sums, "narrow", scatter_dimension=0, tiled=True)
    both = jnp.concatenate(
        gate_terms(sums[:, :hidden], sums[:, hidden : 2 * hidden], sums[:, 2 * hidden :]), axis=1
    )
    both = lax.all_gather(both, "narrow", axis=0, tiled=True)
    back = dot(both[:, :hidden], gate_weight, NT) + dot(both[:, hidden:], up_weight, NT)
    return lax.psum_scatter(back, "wide", scatter_dimension=0, tiled=True)


def solution(mesh):
    wide, narrow = mesh.shape["wide"], mesh.shape["narrow"]
    near, far = 1, 2

    def swap(x, axis, k):
        return lax.ppermute(x, axis, [(i, i ^ k) for i in range(mesh.shape[axis])])

    def by_swaps(normed, target, own_target, gate_weight, up_weight, down_weight):
        width, hidden = gate_weight.shape
        share = hidden // narrow
        index = lax.axis_index("narrow").astype(jnp.int32).reshape(1)
        pair = [gate_weight, up_weight]
        diagonal = near | far
        targets = [own_target] + [swap(own_target, "wide", k) for k in range(1, wide)]
        normeds = [normed] + [swap(normed, "wide", k) for k in range(1, wide)]

        ahead = rows_ahead(index, down_weight, [near], share)
        ahead, *targets[1:] = lax.optimization_barrier((ahead, *targets[1:]))
        send, keep, held_diagonal = hidden_gradient(
            index, targets, ahead, down_weight, pair, diagonal, [near, diagonal, 0, far], share
        )
        send, *normeds = lax.optimization_barrier((send, *normeds))
        hidden_near = swap(send, "narrow", near)
        (part,) = gate_and_up(index, normeds, held_diagonal, pair, [], share, [send], "gate_up_diagonal")
        part, hidden_near = lax.optimization_barrier((part, hidden_near))
        sum_far = (keep[:, share:] + hidden_near[:, share:].astype(F32)).astype(BF16)
        hidden_far = swap(sum_far, "narrow", far)
        got = swap(part, "narrow", near)
        (part,) = gate_and_up(index, normeds, None, pair, [far], share, [sum_far], "gate_up_far", False)
        part, got, hidden_far = lax.optimization_barrier((part, got, hidden_far))
        sum_far = (part + got).astype(BF16)
        got_far = swap(sum_far, "narrow", far)
        own, part, held = gate_and_up(
            index, normeds, None, pair, [0, near], share, [sum_far], "gate_up_near_own"
        )
        part, got_far = lax.optimization_barrier((part, got_far))
        got = swap(part, "narrow", near)
        rows, held = gate_rows(own, got, got_far, keep, hidden_near, hidden_far, held)

        rows_far = swap(rows, "narrow", far)
        rows_near = swap(rows, "narrow", near)
        total, held = backward(index, [rows, rows_near], held, pair, [far], None, 1, "back_own_near")
        total, rows_far = lax.optimization_barrier((total, rows_far))
        rows_diagonal = swap(rows_far, "narrow", near)
        total, held = backward(index, [rows_far], held, pair, [diagonal], total, 1, "back_far")
        pieces = backward(index, [rows_diagonal], held, pair, [], total, wide, "back_diagonal")
        back_normed, inner = pieces[0][:, :width], pieces[0][:, width : width + 1]
        for k in range(1, wide):
            got = swap(pieces[k], "wide", k)
            back_normed = back_normed + got[:, :width].astype(F32)
            inner = inner + joined(got[:, width:])
        return back_normed, inner

    def on_device(tokens, signs, magnitude, target, norm_gain, gate_weight, up_weight, down_weight):
        width, hidden = gate_weight.shape
        features = width * narrow
        weights = (gate_weight, up_weight, down_weight)
        square = narrow == (near | far) + 1 and hidden % (narrow * LANES) == 0 and wide & (wide - 1) == 0

        delta, latent, squares, gain, own_target = latents(
            tokens, signs, magnitude, norm_gain.reshape(1, -1), target
        )
        if square:
            squares = squares + sum(swap(squares, "narrow", k) for k in range(1, narrow))
        else:
            squares = lax.psum(squares, "narrow")
        scale = lax.rsqrt(squares / features + EPS)
        unit = latent * scale
        normed = (unit * gain).astype(BF16)
        if square:
            back_normed, inner = by_swaps(normed, target, own_target, *weights)
            scaled = back_normed * gain
        else:
            scaled = by_collectives(normed, target, *weights) * gain
            inner = lax.psum(jnp.sum(scaled * unit, axis=1, keepdims=True), "narrow")
        back_latent = scale * (scaled - unit * (inner / features))
        return delta + ASCENT * (own_target.astype(F32) + back_latent)

    rows = P(("groups", "wide"), "narrow")
    in_specs = (rows, rows, rows, rows, P("narrow"), P("narrow", "wide"), P("narrow", "wide"), P("wide", "narrow"))
    return jax.shard_map(on_device, mesh=mesh, in_specs=in_specs, out_specs=rows, check_vma=False)
```

```python
import jax
import jax.numpy as jnp
from jax import lax
from jax.experimental import pallas as pl
from jax.experimental.pallas import tpu as pltpu
from jax.sharding import PartitionSpec as P

EPS = 1e-05
ASCENT = 0.5
LANES = 128
STEP = 512

NN = (((1,), (0,)), ((), ()))
NT = (((1,), (1,)), ((), ()))
ANY = pl.BlockSpec(memory_space=pl.ANY)
HBM = pl.BlockSpec(memory_space=pltpu.HBM)
SMEM = pl.BlockSpec(memory_space=pltpu.SMEM)
VMEM = pl.BlockSpec(memory_space=pltpu.VMEM)
F32 = jnp.float32
BF16 = jnp.bfloat16


def dot(a, b, dims):
    return lax.dot_general(a, b, dims, preferred_element_type=F32)


def steps(length):
    count = next(c for c in range(max(1, length // STEP), length + 1) if length % (c * LANES) == 0)
    return [(i * (length // count), length // count) for i in range(count)]


def params(mebibytes):
    return pltpu.CompilerParams(vmem_limit_bytes=mebibytes << 20)


def in_hbm(arrays):
    return [pltpu.with_memory_space_constraint(x, pltpu.HBM) for x in arrays]


def in_vmem(x):
    return pltpu.with_memory_space_constraint(x, pltpu.VMEM)


def cost(m, k, n):
    return pl.CostEstimate(flops=2 * m * k * n, bytes_accessed=2 * k * n, transcendentals=0)


def split(x):
    high = x.astype(BF16)
    low = (x - high.astype(F32)).astype(BF16)
    return jnp.concatenate([jnp.broadcast_to(y, (x.shape[0], LANES // 2)) for y in (high, low)], axis=1)


def joined(x):
    return x[:, :1].astype(F32) + x[:, LANES // 2 : LANES // 2 + 1].astype(F32)


def bring(index_ref, pick, share, sources, target_ref, place, sems, first=0):
    copies = []
    for at, n in steps(share):
        for i, source in enumerate(sources):
            begin = pl.multiple_of((index_ref[0] ^ pick) * share + at, LANES)
            copies.append(
                pltpu.make_async_copy(
                    source.at[:, pl.ds(begin, n)],
                    target_ref.at[place + i, :, pl.ds(at, n)],
                    sems.at[first + len(copies)],
                )
            )
    return copies


def rows_ahead(index, down_weight, picks, share):
    width = down_weight.shape[1]

    def kernel(index_ref, down_ref, out_ref, sems):
        copies = []
        for r, pick in enumerate(picks):
            begin = pl.multiple_of((index_ref[0] ^ pick) * share, LANES)
            source, target = down_ref.at[pl.ds(begin, share), :], out_ref.at[pl.ds(r * share, share), :]
            copies.append(pltpu.make_async_copy(source, target, sems.at[r]))
        for copy in copies:
            copy.start()
        for copy in copies:
            copy.wait()

    return pl.pallas_call(
        kernel,
        in_specs=[SMEM, HBM],
        out_specs=VMEM,
        out_shape=pltpu.VMEM((len(picks) * share, width), down_weight.dtype),
        scratch_shapes=[pltpu.SemaphoreType.DMA((len(picks),))],
        compiler_params=params(8),
        cost_estimate=cost(8, width, len(picks) * share),
        name="rows_ahead",
    )(index, *in_hbm([down_weight]))


def hidden_gradient(index, blocks, held, down_weight, pair, pick, picks, share):
    size, width = blocks[0].shape
    tokens = size * len(blocks)
    first = held.shape[0] // share
    parts = [(r, at, n) for r in range(first, len(picks)) for at, n in steps(share)]
    n = parts[0][2]
    half = len(picks) // 2 * share

    def kernel(index_ref, *refs):
        block_refs, refs = refs[: len(blocks)], refs[len(blocks) :]
        held_ref, down_ref, refs = refs[0], refs[1], refs[2:]
        pair_refs, refs = refs[: len(pair)], refs[len(pair) :]
        send_ref, keep_ref, next_ref, rows_ref, down_parts, sems, pair_sems = refs
        copies = []
        for j, (r, at, _) in enumerate(parts):
            begin = pl.multiple_of((index_ref[0] ^ picks[r]) * share + at, LANES)
            copies.append(pltpu.make_async_copy(down_ref.at[pl.ds(begin, n), :], down_parts.at[j], sems.at[j]))
        later = bring(index_ref, pick, share, pair_refs, next_ref, 0, pair_sems)
        for copy in copies + later:
            copy.start()
        for p, block in enumerate(block_refs):
            rows_ref[p * size : (p + 1) * size, :] = block[...]

        @pl.loop(0, held.shape[0] // n)
        def _(step):
            here = pl.ds(pl.multiple_of(step * n, n), n)
            send_ref[:, here] = dot(rows_ref[...], held_ref[here, :], NT)

        for j, (r, at, _) in enumerate(parts):
            copies[j].wait()
            here, part = r * share + at, dot(rows_ref[...], down_parts[j], NT)
            if here < half:
                send_ref[:, pl.ds(here, n)] = part
            else:
                keep_ref[:, pl.ds(here - half, n)] = part
        for copy in later:
            copy.wait()

    count = len(steps(share))
    return pl.pallas_call(
        kernel,
        in_specs=[SMEM] + [VMEM] * (len(blocks) + 1) + [HBM] * (1 + len(pair)),
        out_specs=[VMEM] * 3,
        out_shape=[
            jax.ShapeDtypeStruct((tokens, half), F32),
            jax.ShapeDtypeStruct((tokens, half), F32),
            pltpu.VMEM((len(pair), width, share), BF16),
        ],
        scratch_shapes=[
            pltpu.VMEM((tokens, width), BF16),
            pltpu.VMEM((len(parts), n, width), BF16),
            pltpu.SemaphoreType.DMA((len(parts),)),
            pltpu.SemaphoreType.DMA((len(pair) * count,)),
        ],
        compiler_params=params(22),
        cost_estimate=cost(tokens, width, len(picks) * share),
        name="back_hidden",
    )(index, *blocks, in_vmem(held), *in_hbm([down_weight, *pair]))


def gate_and_up(index, blocks, held, pair, picks, share, after, name, stays=True):
    size, width = blocks[0].shape
    tokens = size * len(blocks)
    given = [] if held is None else [held]
    use = held is None
    outs = len(picks) if use else 1
    count = len(steps(share)) * len(pair)

    def kernel(index_ref, *refs):
        block_refs, refs = refs[: len(blocks)], refs[len(blocks) :]
        held_refs, refs = refs[: len(given)], refs[len(given) :]
        pair_refs, refs = refs[: len(pair)], refs[len(pair) + len(after) :]
        out_refs, (*next_ref, rows_ref, sems) = refs[:outs], refs[outs:]
        copies = []
        for k, pick in enumerate(picks):
            copies += bring(index_ref, pick, share, pair_refs, next_ref[0], k * len(pair), sems, k * count)
        for copy in copies:
            copy.start()
        for p, block in enumerate(block_refs):
            rows_ref[p * size : (p + 1) * size, :] = block[...]
        n = steps(share)[0][1]
        for held_ref, out in zip(held_refs, out_refs):

            @pl.loop(0, share // n)
            def _(step):
                for i in range(len(pair)):
                    part = dot(rows_ref[...], held_ref[i, :, pl.ds(pl.multiple_of(step * n, n), n)], NN)
                    out[:, pl.ds(pl.multiple_of(i * share + step * n, LANES), n)] = part

        for j, copy in enumerate(copies):
            copy.wait()
            if use:
                k, (at, n), i = j // count, steps(share)[j % count // len(pair)], j % len(pair)
                part = dot(rows_ref[...], next_ref[0][k * len(pair) + i, :, pl.ds(at, n)], NN)
                out_refs[k][:, pl.ds(i * share + at, n)] = part.astype(out_refs[k].dtype)

    brought = [pltpu.VMEM((len(pair) * len(picks), width, share), BF16)] if picks else []
    more, scratch = (brought, []) if stays else ([], brought)
    return pl.pallas_call(
        kernel,
        in_specs=[SMEM] + [VMEM] * (len(blocks) + len(given)) + [HBM] * len(pair) + [ANY] * len(after),
        out_specs=[VMEM] * (outs + len(more)),
        out_shape=[jax.ShapeDtypeStruct((tokens, len(pair) * share), BF16 if i else F32) for i in range(outs)] + more,
        scratch_shapes=scratch
        + [
            pltpu.VMEM((tokens, width), BF16),
            pltpu.SemaphoreType.DMA((max(1, count * len(picks)),)),
        ],
        compiler_params=params(8 if stays else 20),
        cost_estimate=cost(tokens, width, outs * len(pair) * share),
        name=name,
    )(index, *blocks, *[in_vmem(h) for h in given], *in_hbm(pair), *after)


def backward(index, rows, held, pair, picks, before, pieces, name):
    tokens = rows[0].shape[0]
    _, width, share = held.shape
    size = tokens // pieces
    extra = [] if before is None else [before]
    count = len(steps(share)) * len(pair)
    n = steps(width)[0][1]

    def kernel(index_ref, *refs):
        row_refs, refs = refs[: len(rows)], refs[len(rows) :]
        held_ref, refs = refs[0], refs[1:]
        before_refs, refs = refs[: len(extra)], refs[len(extra) :]
        pair_refs, refs = refs[: len(pair)], refs[len(pair) :]
        out_refs, refs = refs[:pieces], refs[pieces:]
        copies = []
        for k, pick in enumerate(picks):
            copies += bring(index_ref, pick, share, pair_refs, refs[0], k * len(pair), refs[1], k * count)
        for copy in copies:
            copy.start()
        inner = sum(joined(r[:, pl.ds(2 * share, LANES)]) for r in row_refs)
        for b in before_refs:
            inner += b[:, pl.ds(width, 1)]
        for p, out in enumerate(out_refs):
            mine = inner[p * size : (p + 1) * size]
            out[:, pl.ds(width, LANES)] = split(mine) if p else jnp.broadcast_to(mine, (size, LANES))

        @pl.loop(0, width // n)
        def _(step):
            here = pl.ds(pl.multiple_of(step * n, n), n)
            part = sum(
                dot(row_refs[j // 2][:, pl.ds(j % 2 * share, share)], held_ref[j, here, :], NT)
                for j in range(2 * len(rows))
            )
            for b in before_refs:
                part += b[:, here]
            for p, out in enumerate(out_refs):
                out[:, here] = part[p * size : (p + 1) * size].astype(out.dtype)

        for copy in copies:
            copy.wait()

    more = [pltpu.VMEM((len(pair) * len(picks), width, share), BF16)] if picks else []
    return pl.pallas_call(
        kernel,
        in_specs=[SMEM] + [VMEM] * (len(rows) + 1 + len(extra)) + [HBM] * len(pair),
        out_specs=[VMEM] * (pieces + len(more)),
        out_shape=[jax.ShapeDtypeStruct((size, width + LANES), BF16 if p else F32) for p in range(pieces)] + more,
        scratch_shapes=[pltpu.SemaphoreType.DMA((max(1, count * len(picks)),))],
        compiler_params=params(8),
        cost_estimate=cost(tokens, held.shape[0] * share, width),
        name=name,
    )(index, *rows, in_vmem(held), *extra, *in_hbm(pair))


def latents(tokens, signs, magnitude, gain, target):
    given = (tokens, signs, magnitude)

    def kernel(*refs):
        sources, (delta_ref, latent_ref, squares_ref, *same_refs), scratch = refs[:5], refs[5:10], refs[10:]
        copies = [
            pltpu.make_async_copy(source, target, scratch[-1].at[i])
            for i, (source, target) in enumerate(zip(sources, (*scratch[:-1], *same_refs)))
        ]
        for copy in copies:
            copy.start()
        for copy in copies[: len(given)]:
            copy.wait()
        delta = (2 * scratch[1][...] - 1).astype(F32) * scratch[2][...]
        latent = scratch[0][...].astype(F32) + delta
        delta_ref[...] = delta
        latent_ref[...] = latent
        squares_ref[...] = jnp.sum(latent * latent, axis=1, keepdims=True)
        for copy in copies[len(given) :]:
            copy.wait()

    whole = jax.ShapeDtypeStruct(tokens.shape, F32)
    return pl.pallas_call(
        kernel,
        in_specs=[HBM] * 5,
        out_specs=[VMEM] * 5,
        out_shape=[
            whole,
            whole,
            jax.ShapeDtypeStruct((tokens.shape[0], 1), F32),
            jax.ShapeDtypeStruct(gain.shape, F32),
            jax.ShapeDtypeStruct(target.shape, target.dtype),
        ],
        scratch_shapes=[pltpu.VMEM(x.shape, x.dtype) for x in given] + [pltpu.SemaphoreType.DMA((5,))],
        compiler_params=params(8),
        cost_estimate=pl.CostEstimate(flops=8 * tokens.size, bytes_accessed=18 * tokens.size, transcendentals=0),
        name="latents",
    )(*in_hbm([*given, gain, target]))


def gate_terms(gate, up, back_hidden):
    sig = jax.nn.sigmoid(gate)
    back_gate = (back_hidden * up * sig * (1.0 + gate * (1.0 - sig))).astype(BF16)
    back_up = (back_hidden * gate * sig).astype(BF16)
    return back_gate, back_up


def gate_rows(own, got_near, got_far, hidden_own, hidden_near, hidden_far, held):
    tokens, share = hidden_far.shape

    def kernel(own_ref, near_ref, far_ref, hidden_own_ref, hidden_near_ref, hidden_far_ref, _, rows_ref, __):
        inner = jnp.zeros((tokens, 1), F32)
        for at, n in steps(share):
            here, there = pl.ds(at, n), pl.ds(share + at, n)
            gate, up = (
                own_ref[:, x] + near_ref[:, x].astype(F32) + far_ref[:, x].astype(F32) for x in (here, there)
            )
            back_hidden = hidden_own_ref[:, here] + hidden_near_ref[:, here].astype(F32)
            back_hidden += hidden_far_ref[:, here].astype(F32)
            back_gate, back_up = gate_terms(gate, up, back_hidden)
            rows_ref[:, here] = back_gate
            rows_ref[:, there] = back_up
            products = back_gate.astype(F32) * gate + back_up.astype(F32) * up
            inner += jnp.sum(products, axis=1, keepdims=True)
        rows_ref[:, pl.ds(2 * share, LANES)] = split(inner)

    return pl.pallas_call(
        kernel,
        in_specs=[VMEM] * 7,
        out_specs=[VMEM] * 2,
        out_shape=[
            jax.ShapeDtypeStruct((tokens, 2 * share + LANES), BF16),
            pltpu.VMEM(held.shape, held.dtype),
        ],
        input_output_aliases={6: 1},
        compiler_params=params(8),
        cost_estimate=pl.CostEstimate(
            flops=20 * tokens * share, bytes_accessed=30 * tokens * share, transcendentals=tokens * share
        ),
        name="gate",
    )(own, got_near, got_far, hidden_own, hidden_near, hidden_far, in_vmem(held))


def by_collectives(normed, target, gate_weight, up_weight, down_weight):
    stacked = jnp.stack([normed, target], axis=0)
    rows = lax.all_gather(stacked, "wide", axis=1, tiled=True)
    hidden = gate_weight.shape[1]
    sums = jnp.concatenate(
        [dot(rows[0], gate_weight, NN), dot(rows[0], up_weight, NN), dot(rows[1], down_weight, NT)], axis=1
    )
    sums = lax.psum_scatter(sums, "narrow", scatter_dimension=0, tiled=True)
    both = jnp.concatenate(
        gate_terms(sums[:, :hidden], sums[:, hidden : 2 * hidden], sums[:, 2 * hidden :]), axis=1
    )
    both = lax.all_gather(both, "narrow", axis=0, tiled=True)
    back = dot(both[:, :hidden], gate_weight, NT) + dot(both[:, hidden:], up_weight, NT)
    return lax.psum_scatter(back, "wide", scatter_dimension=0, tiled=True)


def solution(mesh):
    wide, narrow = mesh.shape["wide"], mesh.shape["narrow"]
    near, far = 1, 2

    def swap(x, axis, k):
        return lax.ppermute(x, axis, [(i, i ^ k) for i in range(mesh.shape[axis])])

    def turn(x, k):
        return lax.ppermute(x, "wide", [(i, (i + k) % wide) for i in range(wide)])

    def by_swaps(normed, target, own_target, gate_weight, up_weight, down_weight):
        width, hidden = gate_weight.shape
        share = hidden // narrow
        index = lax.axis_index("narrow").astype(jnp.int32).reshape(1)
        pair = [gate_weight, up_weight]
        diagonal = near | far
        targets = [own_target] + [swap(own_target, "wide", k) for k in range(1, wide)]
        normeds = [normed] + [swap(normed, "wide", k) for k in range(1, wide)]

        ahead = rows_ahead(index, down_weight, [near], share)
        ahead, *targets[1:] = lax.optimization_barrier((ahead, *targets[1:]))
        send, keep, held_diagonal = hidden_gradient(
            index, targets, ahead, down_weight, pair, diagonal, [near, diagonal, 0, far], share
        )
        send, *normeds = lax.optimization_barrier((send, *normeds))
        hidden_near = swap(send, "narrow", near)
        (part,) = gate_and_up(index, normeds, held_diagonal, pair, [], share, [send], "gate_up_diagonal")
        part, hidden_near = lax.optimization_barrier((part, hidden_near))
        sum_far = (keep[:, share:] + hidden_near[:, share:].astype(F32)).astype(BF16)
        hidden_far = swap(sum_far, "narrow", far)
        got = swap(part, "narrow", near)
        (part,) = gate_and_up(index, normeds, None, pair, [far], share, [sum_far], "gate_up_far", False)
        part, got, hidden_far = lax.optimization_barrier((part, got, hidden_far))
        sum_far = (part + got).astype(BF16)
        got_far = swap(sum_far, "narrow", far)
        own, part, held = gate_and_up(
            index, normeds, None, pair, [0, near], share, [sum_far], "gate_up_near_own"
        )
        part, got_far = lax.optimization_barrier((part, got_far))
        got = swap(part, "narrow", near)
        rows, held = gate_rows(own, got, got_far, keep, hidden_near, hidden_far, held)

        rows_far = swap(rows, "narrow", far)
        rows_near = swap(rows, "narrow", near)
        total, held = backward(index, [rows, rows_near], held, pair, [far], None, 1, "back_own_near")
        total, rows_far = lax.optimization_barrier((total, rows_far))
        rows_diagonal = swap(rows_far, "narrow", near)
        total, held = backward(index, [rows_far], held, pair, [diagonal], total, 1, "back_far")
        pieces = backward(index, [rows_diagonal], held, pair, [], total, wide, "back_diagonal")
        back_normed, inner = pieces[0][:, :width], pieces[0][:, width : width + 1]
        for k in reversed(range(1, wide)):
            got = swap(pieces[k], "wide", k)
            back_normed = back_normed + got[:, :width].astype(F32)
            inner = inner + joined(got[:, width:])
        return back_normed, inner

    def on_device(tokens, signs, magnitude, target, norm_gain, gate_weight, up_weight, down_weight):
        width, hidden = gate_weight.shape
        features = width * narrow
        weights = (gate_weight, up_weight, down_weight)
        square = narrow == (near | far) + 1 and hidden % (narrow * LANES) == 0 and wide & (wide - 1) == 0

        delta, latent, squares, gain, own_target = latents(
            tokens, signs, magnitude, norm_gain.reshape(1, -1), target
        )
        if square:
            squares = squares + sum(swap(squares, "narrow", k) for k in range(1, narrow))
        else:
            squares = lax.psum(squares, "narrow")
        scale = lax.rsqrt(squares / features + EPS)
        unit = latent * scale
        normed = (unit * gain).astype(BF16)
        if square:
            back_normed, inner = by_swaps(normed, target, own_target, *weights)
            scaled = back_normed * gain
        else:
            scaled = by_collectives(normed, target, *weights) * gain
            inner = lax.psum(jnp.sum(scaled * unit, axis=1, keepdims=True), "narrow")
        back_latent = scale * (scaled - unit * (inner / features))
        return delta + ASCENT * (own_target.astype(F32) + back_latent)

    rows = P(("groups", "wide"), "narrow")
    in_specs = (rows, rows, rows, rows, P("narrow"), P("narrow", "wide"), P("narrow", "wide"), P("wide", "narrow"))
    return jax.shard_map(on_device, mesh=mesh, in_specs=in_specs, out_specs=rows, check_vma=False)
```

```python
import jax
import jax.numpy as jnp
from jax import lax
from jax.experimental import pallas as pl
from jax.experimental.pallas import tpu as pltpu
from jax.sharding import PartitionSpec as P

EPS = 1e-05
ASCENT = 0.5
LANES = 128
STEP = 512

NN = (((1,), (0,)), ((), ()))
NT = (((1,), (1,)), ((), ()))
ANY = pl.BlockSpec(memory_space=pl.ANY)
HBM = pl.BlockSpec(memory_space=pltpu.HBM)
SMEM = pl.BlockSpec(memory_space=pltpu.SMEM)
VMEM = pl.BlockSpec(memory_space=pltpu.VMEM)
F32 = jnp.float32
BF16 = jnp.bfloat16


def dot(a, b, dims):
    return lax.dot_general(a, b, dims, preferred_element_type=F32)


def steps(length):
    count = next(c for c in range(max(1, length // STEP), length + 1) if length % (c * LANES) == 0)
    return [(i * (length // count), length // count) for i in range(count)]


def params(mebibytes):
    return pltpu.CompilerParams(vmem_limit_bytes=mebibytes << 20)


def in_hbm(arrays):
    return [pltpu.with_memory_space_constraint(x, pltpu.HBM) for x in arrays]


def in_vmem(x):
    return pltpu.with_memory_space_constraint(x, pltpu.VMEM)


def cost(m, k, n):
    return pl.CostEstimate(flops=2 * m * k * n, bytes_accessed=2 * k * n, transcendentals=0)


def split(x):
    high = x.astype(BF16)
    low = (x - high.astype(F32)).astype(BF16)
    return jnp.concatenate([jnp.broadcast_to(y, (x.shape[0], LANES // 2)) for y in (high, low)], axis=1)


def joined(x):
    return x[:, :1].astype(F32) + x[:, LANES // 2 : LANES // 2 + 1].astype(F32)


def bring(index_ref, pick, share, sources, target_ref, place, sems, first=0):
    copies = []
    for at, n in steps(share):
        for i, source in enumerate(sources):
            begin = pl.multiple_of((index_ref[0] ^ pick) * share + at, LANES)
            copies.append(
                pltpu.make_async_copy(
                    source.at[:, pl.ds(begin, n)],
                    target_ref.at[place + i, :, pl.ds(at, n)],
                    sems.at[first + len(copies)],
                )
            )
    return copies


def rows_ahead(index, down_weight, picks, share):
    width = down_weight.shape[1]

    def kernel(index_ref, down_ref, out_ref, sems):
        copies = []
        for r, pick in enumerate(picks):
            begin = pl.multiple_of((index_ref[0] ^ pick) * share, LANES)
            source, target = down_ref.at[pl.ds(begin, share), :], out_ref.at[pl.ds(r * share, share), :]
            copies.append(pltpu.make_async_copy(source, target, sems.at[r]))
        for copy in copies:
            copy.start()
        for copy in copies:
            copy.wait()

    return pl.pallas_call(
        kernel,
        in_specs=[SMEM, HBM],
        out_specs=VMEM,
        out_shape=pltpu.VMEM((len(picks) * share, width), down_weight.dtype),
        scratch_shapes=[pltpu.SemaphoreType.DMA((len(picks),))],
        compiler_params=params(8),
        cost_estimate=cost(8, width, len(picks) * share),
        name="rows_ahead",
    )(index, *in_hbm([down_weight]))


def hidden_gradient(index, blocks, held, down_weight, pair, pick, picks, share):
    size, width = blocks[0].shape
    tokens = size * len(blocks)
    first = held.shape[0] // share
    parts = [(r, at, n) for r in range(first, len(picks)) for at, n in steps(share)]
    n = parts[0][2]
    half = len(picks) // 2 * share

    def kernel(index_ref, *refs):
        block_refs, refs = refs[: len(blocks)], refs[len(blocks) :]
        held_ref, down_ref, refs = refs[0], refs[1], refs[2:]
        pair_refs, refs = refs[: len(pair)], refs[len(pair) :]
        send_ref, keep_ref, next_ref, rows_ref, down_parts, sems, pair_sems = refs
        copies = []
        for j, (r, at, _) in enumerate(parts):
            begin = pl.multiple_of((index_ref[0] ^ picks[r]) * share + at, LANES)
            copies.append(pltpu.make_async_copy(down_ref.at[pl.ds(begin, n), :], down_parts.at[j], sems.at[j]))
        later = bring(index_ref, pick, share, pair_refs, next_ref, 0, pair_sems)
        for copy in copies + later:
            copy.start()
        for p, block in enumerate(block_refs):
            rows_ref[p * size : (p + 1) * size, :] = block[...]

        @pl.loop(0, held.shape[0] // n)
        def _(step):
            here = pl.ds(pl.multiple_of(step * n, n), n)
            send_ref[:, here] = dot(rows_ref[...], held_ref[here, :], NT)

        for j, (r, at, _) in enumerate(parts):
            copies[j].wait()
            here, part = r * share + at, dot(rows_ref[...], down_parts[j], NT)
            if here < half:
                send_ref[:, pl.ds(here, n)] = part
            else:
                keep_ref[:, pl.ds(here - half, n)] = part
        for copy in later:
            copy.wait()

    count = len(steps(share))
    return pl.pallas_call(
        kernel,
        in_specs=[SMEM] + [VMEM] * (len(blocks) + 1) + [HBM] * (1 + len(pair)),
        out_specs=[VMEM] * 3,
        out_shape=[
            jax.ShapeDtypeStruct((tokens, half), F32),
            jax.ShapeDtypeStruct((tokens, half), F32),
            pltpu.VMEM((len(pair), width, share), BF16),
        ],
        scratch_shapes=[
            pltpu.VMEM((tokens, width), BF16),
            pltpu.VMEM((len(parts), n, width), BF16),
            pltpu.SemaphoreType.DMA((len(parts),)),
            pltpu.SemaphoreType.DMA((len(pair) * count,)),
        ],
        compiler_params=params(22),
        cost_estimate=cost(tokens, width, len(picks) * share),
        name="back_hidden",
    )(index, *blocks, in_vmem(held), *in_hbm([down_weight, *pair]))


def gate_and_up(index, blocks, held, pair, picks, share, after, name, stays=True):
    size, width = blocks[0].shape
    tokens = size * len(blocks)
    given = [] if held is None else [held]
    use = held is None
    outs = len(picks) if use else 1
    count = len(steps(share)) * len(pair)

    def kernel(index_ref, *refs):
        block_refs, refs = refs[: len(blocks)], refs[len(blocks) :]
        held_refs, refs = refs[: len(given)], refs[len(given) :]
        pair_refs, refs = refs[: len(pair)], refs[len(pair) + len(after) :]
        out_refs, (*next_ref, rows_ref, sems) = refs[:outs], refs[outs:]
        copies = []
        for k, pick in enumerate(picks):
            copies += bring(index_ref, pick, share, pair_refs, next_ref[0], k * len(pair), sems, k * count)
        for copy in copies:
            copy.start()
        for p, block in enumerate(block_refs):
            rows_ref[p * size : (p + 1) * size, :] = block[...]
        n = steps(share)[0][1]
        for held_ref, out in zip(held_refs, out_refs):

            @pl.loop(0, share // n)
            def _(step):
                for i in range(len(pair)):
                    part = dot(rows_ref[...], held_ref[i, :, pl.ds(pl.multiple_of(step * n, n), n)], NN)
                    out[:, pl.ds(pl.multiple_of(i * share + step * n, LANES), n)] = part

        for j, copy in enumerate(copies):
            copy.wait()
            if use:
                k, (at, n), i = j // count, steps(share)[j % count // len(pair)], j % len(pair)
                part = dot(rows_ref[...], next_ref[0][k * len(pair) + i, :, pl.ds(at, n)], NN)
                out_refs[k][:, pl.ds(i * share + at, n)] = part.astype(out_refs[k].dtype)

    brought = [pltpu.VMEM((len(pair) * len(picks), width, share), BF16)] if picks else []
    more, scratch = (brought, []) if stays else ([], brought)
    return pl.pallas_call(
        kernel,
        in_specs=[SMEM] + [VMEM] * (len(blocks) + len(given)) + [HBM] * len(pair) + [ANY] * len(after),
        out_specs=[VMEM] * (outs + len(more)),
        out_shape=[jax.ShapeDtypeStruct((tokens, len(pair) * share), BF16 if i else F32) for i in range(outs)] + more,
        scratch_shapes=scratch
        + [
            pltpu.VMEM((tokens, width), BF16),
            pltpu.SemaphoreType.DMA((max(1, count * len(picks)),)),
        ],
        compiler_params=params(8 if stays else 20),
        cost_estimate=cost(tokens, width, outs * len(pair) * share),
        name=name,
    )(index, *blocks, *[in_vmem(h) for h in given], *in_hbm(pair), *after)


def backward(index, rows, held, pair, picks, before, pieces, name):
    tokens = rows[0].shape[0]
    _, width, share = held.shape
    size = tokens // pieces
    extra = [] if before is None else [before]
    count = len(steps(share)) * len(pair)
    n = width // 2 if picks and width % (2 * LANES) == 0 else width

    def kernel(index_ref, *refs):
        row_refs, refs = refs[: len(rows)], refs[len(rows) :]
        held_ref, refs = refs[0], refs[1:]
        before_refs, refs = refs[: len(extra)], refs[len(extra) :]
        pair_refs, refs = refs[: len(pair)], refs[len(pair) :]
        out_refs, refs = refs[:pieces], refs[pieces:]
        copies = []
        for k, pick in enumerate(picks):
            copies += bring(index_ref, pick, share, pair_refs, refs[0], k * len(pair), refs[1], k * count)
        for copy in copies:
            copy.start()
        inner = sum(joined(r[:, pl.ds(2 * share, LANES)]) for r in row_refs)
        for b in before_refs:
            inner += b[:, pl.ds(width, 1)]
        for p, out in enumerate(out_refs):
            mine = inner[p * size : (p + 1) * size]
            out[:, pl.ds(width, LANES)] = split(mine) if p else jnp.broadcast_to(mine, (size, LANES))

        @pl.loop(0, width // n)
        def _(step):
            here = pl.ds(pl.multiple_of(step * n, n), n)
            part = sum(
                dot(row_refs[j // 2][:, pl.ds(j % 2 * share, share)], held_ref[j, here, :], NT)
                for j in range(2 * len(rows))
            )
            for b in before_refs:
                part += b[:, here]
            for p, out in enumerate(out_refs):
                out[:, here] = part[p * size : (p + 1) * size].astype(out.dtype)

        for copy in copies:
            copy.wait()

    more = [pltpu.VMEM((len(pair) * len(picks), width, share), BF16)] if picks else []
    return pl.pallas_call(
        kernel,
        in_specs=[SMEM] + [VMEM] * (len(rows) + 1 + len(extra)) + [HBM] * len(pair),
        out_specs=[VMEM] * (pieces + len(more)),
        out_shape=[jax.ShapeDtypeStruct((size, width + LANES), BF16 if p else F32) for p in range(pieces)] + more,
        scratch_shapes=[pltpu.SemaphoreType.DMA((max(1, count * len(picks)),))],
        compiler_params=params(8),
        cost_estimate=cost(tokens, held.shape[0] * share, width),
        name=name,
    )(index, *rows, in_vmem(held), *extra, *in_hbm(pair))


def latents(tokens, signs, magnitude, gain, target):
    given = (tokens, signs, magnitude)

    def kernel(*refs):
        sources, (delta_ref, latent_ref, squares_ref, *same_refs), scratch = refs[:5], refs[5:10], refs[10:]
        copies = [
            pltpu.make_async_copy(source, target, scratch[-1].at[i])
            for i, (source, target) in enumerate(zip(sources, (*scratch[:-1], *same_refs)))
        ]
        for copy in copies:
            copy.start()
        for copy in copies[: len(given)]:
            copy.wait()
        delta = (2 * scratch[1][...] - 1).astype(F32) * scratch[2][...]
        latent = scratch[0][...].astype(F32) + delta
        delta_ref[...] = delta
        latent_ref[...] = latent
        squares_ref[...] = jnp.sum(latent * latent, axis=1, keepdims=True)
        for copy in copies[len(given) :]:
            copy.wait()

    whole = jax.ShapeDtypeStruct(tokens.shape, F32)
    return pl.pallas_call(
        kernel,
        in_specs=[HBM] * 5,
        out_specs=[VMEM] * 5,
        out_shape=[
            whole,
            whole,
            jax.ShapeDtypeStruct((tokens.shape[0], 1), F32),
            jax.ShapeDtypeStruct(gain.shape, F32),
            jax.ShapeDtypeStruct(target.shape, target.dtype),
        ],
        scratch_shapes=[pltpu.VMEM(x.shape, x.dtype) for x in given] + [pltpu.SemaphoreType.DMA((5,))],
        compiler_params=params(8),
        cost_estimate=pl.CostEstimate(flops=8 * tokens.size, bytes_accessed=18 * tokens.size, transcendentals=0),
        name="latents",
    )(*in_hbm([*given, gain, target]))


def gate_terms(gate, up, back_hidden):
    sig = jax.nn.sigmoid(gate)
    back_gate = (back_hidden * up * sig * (1.0 + gate * (1.0 - sig))).astype(BF16)
    back_up = (back_hidden * gate * sig).astype(BF16)
    return back_gate, back_up


def gate_rows(own, got_near, got_far, hidden_own, hidden_near, hidden_far, held):
    tokens, share = hidden_far.shape

    def kernel(own_ref, near_ref, far_ref, hidden_own_ref, hidden_near_ref, hidden_far_ref, _, rows_ref, __):
        inner = jnp.zeros((tokens, 1), F32)
        for at, n in steps(share):
            here, there = pl.ds(at, n), pl.ds(share + at, n)
            gate, up = (
                own_ref[:, x] + near_ref[:, x].astype(F32) + far_ref[:, x].astype(F32) for x in (here, there)
            )
            back_hidden = hidden_own_ref[:, here] + hidden_near_ref[:, here].astype(F32)
            back_hidden += hidden_far_ref[:, here].astype(F32)
            back_gate, back_up = gate_terms(gate, up, back_hidden)
            rows_ref[:, here] = back_gate
            rows_ref[:, there] = back_up
            products = back_gate.astype(F32) * gate + back_up.astype(F32) * up
            inner += jnp.sum(products, axis=1, keepdims=True)
        rows_ref[:, pl.ds(2 * share, LANES)] = split(inner)

    return pl.pallas_call(
        kernel,
        in_specs=[VMEM] * 7,
        out_specs=[VMEM] * 2,
        out_shape=[
            jax.ShapeDtypeStruct((tokens, 2 * share + LANES), BF16),
            pltpu.VMEM(held.shape, held.dtype),
        ],
        input_output_aliases={6: 1},
        compiler_params=params(8),
        cost_estimate=pl.CostEstimate(
            flops=20 * tokens * share, bytes_accessed=30 * tokens * share, transcendentals=tokens * share
        ),
        name="gate",
    )(own, got_near, got_far, hidden_own, hidden_near, hidden_far, in_vmem(held))


def by_collectives(normed, target, gate_weight, up_weight, down_weight):
    stacked = jnp.stack([normed, target], axis=0)
    rows = lax.all_gather(stacked, "wide", axis=1, tiled=True)
    hidden = gate_weight.shape[1]
    sums = jnp.concatenate(
        [dot(rows[0], gate_weight, NN), dot(rows[0], up_weight, NN), dot(rows[1], down_weight, NT)], axis=1
    )
    sums = lax.psum_scatter(sums, "narrow", scatter_dimension=0, tiled=True)
    both = jnp.concatenate(
        gate_terms(sums[:, :hidden], sums[:, hidden : 2 * hidden], sums[:, 2 * hidden :]), axis=1
    )
    both = lax.all_gather(both, "narrow", axis=0, tiled=True)
    back = dot(both[:, :hidden], gate_weight, NT) + dot(both[:, hidden:], up_weight, NT)
    return lax.psum_scatter(back, "wide", scatter_dimension=0, tiled=True)


def solution(mesh):
    wide, narrow = mesh.shape["wide"], mesh.shape["narrow"]
    near, far = 1, 2

    def swap(x, axis, k):
        return lax.ppermute(x, axis, [(i, i ^ k) for i in range(mesh.shape[axis])])

    def turn(x, k):
        return lax.ppermute(x, "wide", [(i, (i + k) % wide) for i in range(wide)])

    def by_swaps(normed, target, own_target, gate_weight, up_weight, down_weight):
        width, hidden = gate_weight.shape
        share = hidden // narrow
        index = lax.axis_index("narrow").astype(jnp.int32).reshape(1)
        pair = [gate_weight, up_weight]
        diagonal = near | far
        targets = [own_target] + [swap(own_target, "wide", k) for k in range(1, wide)]
        normeds = [normed] + [swap(normed, "wide", k) for k in range(1, wide)]

        ahead = rows_ahead(index, down_weight, [near], share)
        ahead, *targets[1:] = lax.optimization_barrier((ahead, *targets[1:]))
        send, keep, held_diagonal = hidden_gradient(
            index, targets, ahead, down_weight, pair, diagonal, [near, diagonal, 0, far], share
        )
        send, *normeds = lax.optimization_barrier((send, *normeds))
        hidden_near = swap(send, "narrow", near)
        (part,) = gate_and_up(index, normeds, held_diagonal, pair, [], share, [send], "gate_up_diagonal")
        part, hidden_near = lax.optimization_barrier((part, hidden_near))
        sum_far = (keep[:, share:] + hidden_near[:, share:].astype(F32)).astype(BF16)
        hidden_far = swap(sum_far, "narrow", far)
        got = swap(part, "narrow", near)
        (part,) = gate_and_up(index, normeds, None, pair, [far], share, [sum_far], "gate_up_far", False)
        part, got, hidden_far = lax.optimization_barrier((part, got, hidden_far))
        sum_far = (part + got).astype(BF16)
        got_far = swap(sum_far, "narrow", far)
        own, part, held = gate_and_up(
            index, normeds, None, pair, [0, near], share, [sum_far], "gate_up_near_own"
        )
        part, got_far = lax.optimization_barrier((part, got_far))
        got = swap(part, "narrow", near)
        rows, held = gate_rows(own, got, got_far, keep, hidden_near, hidden_far, held)

        rows_far = swap(rows, "narrow", far)
        rows_near = swap(rows, "narrow", near)
        total, held = backward(index, [rows, rows_near], held, pair, [far], None, 1, "back_own_near")
        total, rows_far = lax.optimization_barrier((total, rows_far))
        rows_diagonal = swap(rows_far, "narrow", near)
        total, held = backward(index, [rows_far], held, pair, [diagonal], total, 1, "back_far")
        pieces = backward(index, [rows_diagonal], held, pair, [], total, wide, "back_diagonal")
        back_normed, inner = pieces[0][:, :width], pieces[0][:, width : width + 1]
        for k in reversed(range(1, wide)):
            got = swap(pieces[k], "wide", k)
            back_normed = back_normed + got[:, :width].astype(F32)
            inner = inner + joined(got[:, width:])
        return back_normed, inner

    def on_device(tokens, signs, magnitude, target, norm_gain, gate_weight, up_weight, down_weight):
        width, hidden = gate_weight.shape
        features = width * narrow
        weights = (gate_weight, up_weight, down_weight)
        square = narrow == (near | far) + 1 and hidden % (narrow * LANES) == 0 and wide & (wide - 1) == 0

        delta, latent, squares, gain, own_target = latents(
            tokens, signs, magnitude, norm_gain.reshape(1, -1), target
        )
        if square:
            squares = squares + sum(swap(squares, "narrow", k) for k in range(1, narrow))
        else:
            squares = lax.psum(squares, "narrow")
        scale = lax.rsqrt(squares / features + EPS)
        unit = latent * scale
        normed = (unit * gain).astype(BF16)
        if square:
            back_normed, inner = by_swaps(normed, target, own_target, *weights)
            scaled = back_normed * gain
        else:
            scaled = by_collectives(normed, target, *weights) * gain
            inner = lax.psum(jnp.sum(scaled * unit, axis=1, keepdims=True), "narrow")
        back_latent = scale * (scaled - unit * (inner / features))
        return delta + ASCENT * (own_target.astype(F32) + back_latent)

    rows = P(("groups", "wide"), "narrow")
    in_specs = (rows, rows, rows, rows, P("narrow"), P("narrow", "wide"), P("narrow", "wide"), P("wide", "narrow"))
    return jax.shard_map(on_device, mesh=mesh, in_specs=in_specs, out_specs=rows, check_vma=False)
```

```python
import jax
import jax.numpy as jnp
from jax import lax
from jax.experimental import pallas as pl
from jax.experimental.pallas import tpu as pltpu
from jax.sharding import PartitionSpec as P

EPS = 1e-05
ASCENT = 0.5
LANES = 128
STEP = 512

NN = (((1,), (0,)), ((), ()))
NT = (((1,), (1,)), ((), ()))
ANY = pl.BlockSpec(memory_space=pl.ANY)
HBM = pl.BlockSpec(memory_space=pltpu.HBM)
SMEM = pl.BlockSpec(memory_space=pltpu.SMEM)
VMEM = pl.BlockSpec(memory_space=pltpu.VMEM)
F32 = jnp.float32
BF16 = jnp.bfloat16


def dot(a, b, dims):
    return lax.dot_general(a, b, dims, preferred_element_type=F32)


def steps(length):
    count = next(c for c in range(max(1, length // STEP), length + 1) if length % (c * LANES) == 0)
    return [(i * (length // count), length // count) for i in range(count)]


def params(mebibytes):
    return pltpu.CompilerParams(vmem_limit_bytes=mebibytes << 20)


def in_hbm(arrays):
    return [pltpu.with_memory_space_constraint(x, pltpu.HBM) for x in arrays]


def in_vmem(x):
    return pltpu.with_memory_space_constraint(x, pltpu.VMEM)


def cost(m, k, n):
    return pl.CostEstimate(flops=2 * m * k * n, bytes_accessed=2 * k * n, transcendentals=0)


def split(x):
    high = x.astype(BF16)
    low = (x - high.astype(F32)).astype(BF16)
    return jnp.concatenate([jnp.broadcast_to(y, (x.shape[0], LANES // 2)) for y in (high, low)], axis=1)


def joined(x):
    return x[:, :1].astype(F32) + x[:, LANES // 2 : LANES // 2 + 1].astype(F32)


def bring(index_ref, pick, share, sources, target_ref, place, sems, first=0):
    copies = []
    for at, n in steps(share):
        for i, source in enumerate(sources):
            begin = pl.multiple_of((index_ref[0] ^ pick) * share + at, LANES)
            copies.append(
                pltpu.make_async_copy(
                    source.at[:, pl.ds(begin, n)],
                    target_ref.at[place + i, :, pl.ds(at, n)],
                    sems.at[first + len(copies)],
                )
            )
    return copies


def rows_ahead(index, down_weight, picks, share):
    width = down_weight.shape[1]

    def kernel(index_ref, down_ref, out_ref, sems):
        copies = []
        for r, pick in enumerate(picks):
            begin = pl.multiple_of((index_ref[0] ^ pick) * share, LANES)
            source, target = down_ref.at[pl.ds(begin, share), :], out_ref.at[pl.ds(r * share, share), :]
            copies.append(pltpu.make_async_copy(source, target, sems.at[r]))
        for copy in copies:
            copy.start()
        for copy in copies:
            copy.wait()

    return pl.pallas_call(
        kernel,
        in_specs=[SMEM, HBM],
        out_specs=VMEM,
        out_shape=pltpu.VMEM((len(picks) * share, width), down_weight.dtype),
        scratch_shapes=[pltpu.SemaphoreType.DMA((len(picks),))],
        compiler_params=params(8),
        cost_estimate=cost(8, width, len(picks) * share),
        name="rows_ahead",
    )(index, *in_hbm([down_weight]))


def hidden_gradient(index, blocks, held, down_weight, pair, pick, picks, share):
    size, width = blocks[0].shape
    tokens = size * len(blocks)
    first = held.shape[0] // share
    parts = [(r, at, n) for r in range(first, len(picks)) for at, n in steps(share)]
    n = parts[0][2]
    half = len(picks) // 2 * share

    def kernel(index_ref, *refs):
        block_refs, refs = refs[: len(blocks)], refs[len(blocks) :]
        held_ref, down_ref, refs = refs[0], refs[1], refs[2:]
        pair_refs, refs = refs[: len(pair)], refs[len(pair) :]
        send_ref, keep_ref, next_ref, rows_ref, down_parts, sems, pair_sems = refs
        copies = []
        for j, (r, at, _) in enumerate(parts):
            begin = pl.multiple_of((index_ref[0] ^ picks[r]) * share + at, LANES)
            copies.append(pltpu.make_async_copy(down_ref.at[pl.ds(begin, n), :], down_parts.at[j], sems.at[j]))
        later = bring(index_ref, pick, share, pair_refs, next_ref, 0, pair_sems)
        for copy in copies + later:
            copy.start()
        for p, block in enumerate(block_refs):
            rows_ref[p * size : (p + 1) * size, :] = block[...]

        @pl.loop(0, held.shape[0] // n)
        def _(step):
            here = pl.ds(pl.multiple_of(step * n, n), n)
            send_ref[:, here] = dot(rows_ref[...], held_ref[here, :], NT)

        for j, (r, at, _) in enumerate(parts):
            copies[j].wait()
            here, part = r * share + at, dot(rows_ref[...], down_parts[j], NT)
            if here < half:
                send_ref[:, pl.ds(here, n)] = part
            else:
                keep_ref[:, pl.ds(here - half, n)] = part
        for copy in later:
            copy.wait()

    count = len(steps(share))
    return pl.pallas_call(
        kernel,
        in_specs=[SMEM] + [VMEM] * (len(blocks) + 1) + [HBM] * (1 + len(pair)),
        out_specs=[VMEM] * 3,
        out_shape=[
            jax.ShapeDtypeStruct((tokens, half), F32),
            jax.ShapeDtypeStruct((tokens, half), F32),
            pltpu.VMEM((len(pair), width, share), BF16),
        ],
        scratch_shapes=[
            pltpu.VMEM((tokens, width), BF16),
            pltpu.VMEM((len(parts), n, width), BF16),
            pltpu.SemaphoreType.DMA((len(parts),)),
            pltpu.SemaphoreType.DMA((len(pair) * count,)),
        ],
        compiler_params=params(22),
        cost_estimate=cost(tokens, width, len(picks) * share),
        name="back_hidden",
    )(index, *blocks, in_vmem(held), *in_hbm([down_weight, *pair]))


def gate_and_up(index, blocks, held, pair, picks, share, after, name, stays=True):
    size, width = blocks[0].shape
    tokens = size * len(blocks)
    given = [] if held is None else [held]
    use = held is None
    outs = len(picks) if use else 1
    count = len(steps(share)) * len(pair)

    def kernel(index_ref, *refs):
        block_refs, refs = refs[: len(blocks)], refs[len(blocks) :]
        held_refs, refs = refs[: len(given)], refs[len(given) :]
        pair_refs, refs = refs[: len(pair)], refs[len(pair) + len(after) :]
        out_refs, (*next_ref, rows_ref, sems) = refs[:outs], refs[outs:]
        copies = []
        for k, pick in enumerate(picks):
            copies += bring(index_ref, pick, share, pair_refs, next_ref[0], k * len(pair), sems, k * count)
        for copy in copies:
            copy.start()
        for p, block in enumerate(block_refs):
            rows_ref[p * size : (p + 1) * size, :] = block[...]
        n = steps(share)[0][1] if picks else share
        for held_ref, out in zip(held_refs, out_refs):

            @pl.loop(0, share // n)
            def _(step):
                for i in range(len(pair)):
                    part = dot(rows_ref[...], held_ref[i, :, pl.ds(pl.multiple_of(step * n, n), n)], NN)
                    out[:, pl.ds(pl.multiple_of(i * share + step * n, LANES), n)] = part

        for j, copy in enumerate(copies):
            copy.wait()
            if use:
                k, (at, n), i = j // count, steps(share)[j % count // len(pair)], j % len(pair)
                part = dot(rows_ref[...], next_ref[0][k * len(pair) + i, :, pl.ds(at, n)], NN)
                out_refs[k][:, pl.ds(i * share + at, n)] = part.astype(out_refs[k].dtype)

    brought = [pltpu.VMEM((len(pair) * len(picks), width, share), BF16)] if picks else []
    more, scratch = (brought, []) if stays else ([], brought)
    return pl.pallas_call(
        kernel,
        in_specs=[SMEM] + [VMEM] * (len(blocks) + len(given)) + [HBM] * len(pair) + [ANY] * len(after),
        out_specs=[VMEM] * (outs + len(more)),
        out_shape=[jax.ShapeDtypeStruct((tokens, len(pair) * share), BF16 if i else F32) for i in range(outs)] + more,
        scratch_shapes=scratch
        + [
            pltpu.VMEM((tokens, width), BF16),
            pltpu.SemaphoreType.DMA((max(1, count * len(picks)),)),
        ],
        compiler_params=params(8 if stays else 20),
        cost_estimate=cost(tokens, width, outs * len(pair) * share),
        name=name,
    )(index, *blocks, *[in_vmem(h) for h in given], *in_hbm(pair), *after)


def backward(index, rows, held, pair, picks, before, pieces, name):
    tokens = rows[0].shape[0]
    _, width, share = held.shape
    size = tokens // pieces
    extra = [] if before is None else [before]
    count = len(steps(share)) * len(pair)
    n = width // 2 if picks and width % (2 * LANES) == 0 else width

    def kernel(index_ref, *refs):
        row_refs, refs = refs[: len(rows)], refs[len(rows) :]
        held_ref, refs = refs[0], refs[1:]
        before_refs, refs = refs[: len(extra)], refs[len(extra) :]
        pair_refs, refs = refs[: len(pair)], refs[len(pair) :]
        out_refs, refs = refs[:pieces], refs[pieces:]
        copies = []
        for k, pick in enumerate(picks):
            copies += bring(index_ref, pick, share, pair_refs, refs[0], k * len(pair), refs[1], k * count)
        for copy in copies:
            copy.start()
        inner = sum(joined(r[:, pl.ds(2 * share, LANES)]) for r in row_refs)
        for b in before_refs:
            inner += b[:, pl.ds(width, 1)]
        for p, out in enumerate(out_refs):
            mine = inner[p * size : (p + 1) * size]
            out[:, pl.ds(width, LANES)] = split(mine) if p else jnp.broadcast_to(mine, (size, LANES))

        @pl.loop(0, width // n)
        def _(step):
            here = pl.ds(pl.multiple_of(step * n, n), n)
            part = sum(
                dot(row_refs[j // 2][:, pl.ds(j % 2 * share, share)], held_ref[j, here, :], NT)
                for j in range(2 * len(rows))
            )
            for b in before_refs:
                part += b[:, here]
            for p, out in enumerate(out_refs):
                out[:, here] = part[p * size : (p + 1) * size].astype(out.dtype)

        for copy in copies:
            copy.wait()

    more = [pltpu.VMEM((len(pair) * len(picks), width, share), BF16)] if picks else []
    return pl.pallas_call(
        kernel,
        in_specs=[SMEM] + [VMEM] * (len(rows) + 1 + len(extra)) + [HBM] * len(pair),
        out_specs=[VMEM] * (pieces + len(more)),
        out_shape=[jax.ShapeDtypeStruct((size, width + LANES), BF16 if p else F32) for p in range(pieces)] + more,
        scratch_shapes=[pltpu.SemaphoreType.DMA((max(1, count * len(picks)),))],
        compiler_params=params(8),
        cost_estimate=cost(tokens, held.shape[0] * share, width),
        name=name,
    )(index, *rows, in_vmem(held), *extra, *in_hbm(pair))


def latents(tokens, signs, magnitude, gain, target):
    given = (tokens, signs, magnitude)

    def kernel(*refs):
        sources, (delta_ref, latent_ref, squares_ref, *same_refs), scratch = refs[:5], refs[5:10], refs[10:]
        copies = [
            pltpu.make_async_copy(source, target, scratch[-1].at[i])
            for i, (source, target) in enumerate(zip(sources, (*scratch[:-1], *same_refs)))
        ]
        for copy in copies:
            copy.start()
        for copy in copies[: len(given)]:
            copy.wait()
        delta = (2 * scratch[1][...] - 1).astype(F32) * scratch[2][...]
        latent = scratch[0][...].astype(F32) + delta
        delta_ref[...] = delta
        latent_ref[...] = latent
        squares_ref[...] = jnp.sum(latent * latent, axis=1, keepdims=True)
        for copy in copies[len(given) :]:
            copy.wait()

    whole = jax.ShapeDtypeStruct(tokens.shape, F32)
    return pl.pallas_call(
        kernel,
        in_specs=[HBM] * 5,
        out_specs=[VMEM] * 5,
        out_shape=[
            whole,
            whole,
            jax.ShapeDtypeStruct((tokens.shape[0], 1), F32),
            jax.ShapeDtypeStruct(gain.shape, F32),
            jax.ShapeDtypeStruct(target.shape, target.dtype),
        ],
        scratch_shapes=[pltpu.VMEM(x.shape, x.dtype) for x in given] + [pltpu.SemaphoreType.DMA((5,))],
        compiler_params=params(8),
        cost_estimate=pl.CostEstimate(flops=8 * tokens.size, bytes_accessed=18 * tokens.size, transcendentals=0),
        name="latents",
    )(*in_hbm([*given, gain, target]))


def gate_terms(gate, up, back_hidden):
    sig = jax.nn.sigmoid(gate)
    back_gate = (back_hidden * up * sig * (1.0 + gate * (1.0 - sig))).astype(BF16)
    back_up = (back_hidden * gate * sig).astype(BF16)
    return back_gate, back_up


def gate_rows(own, got_near, got_far, hidden_own, hidden_near, hidden_far, held):
    tokens, share = hidden_far.shape

    def kernel(own_ref, near_ref, far_ref, hidden_own_ref, hidden_near_ref, hidden_far_ref, _, rows_ref, __):
        inner = jnp.zeros((tokens, 1), F32)
        for at, n in steps(share):
            here, there = pl.ds(at, n), pl.ds(share + at, n)
            gate, up = (
                own_ref[:, x] + near_ref[:, x].astype(F32) + far_ref[:, x].astype(F32) for x in (here, there)
            )
            back_hidden = hidden_own_ref[:, here] + hidden_near_ref[:, here].astype(F32)
            back_hidden += hidden_far_ref[:, here].astype(F32)
            back_gate, back_up = gate_terms(gate, up, back_hidden)
            rows_ref[:, here] = back_gate
            rows_ref[:, there] = back_up
            products = back_gate.astype(F32) * gate + back_up.astype(F32) * up
            inner += jnp.sum(products, axis=1, keepdims=True)
        rows_ref[:, pl.ds(2 * share, LANES)] = split(inner)

    return pl.pallas_call(
        kernel,
        in_specs=[VMEM] * 7,
        out_specs=[VMEM] * 2,
        out_shape=[
            jax.ShapeDtypeStruct((tokens, 2 * share + LANES), BF16),
            pltpu.VMEM(held.shape, held.dtype),
        ],
        input_output_aliases={6: 1},
        compiler_params=params(8),
        cost_estimate=pl.CostEstimate(
            flops=20 * tokens * share, bytes_accessed=30 * tokens * share, transcendentals=tokens * share
        ),
        name="gate",
    )(own, got_near, got_far, hidden_own, hidden_near, hidden_far, in_vmem(held))


def by_collectives(normed, target, gate_weight, up_weight, down_weight):
    stacked = jnp.stack([normed, target], axis=0)
    rows = lax.all_gather(stacked, "wide", axis=1, tiled=True)
    hidden = gate_weight.shape[1]
    sums = jnp.concatenate(
        [dot(rows[0], gate_weight, NN), dot(rows[0], up_weight, NN), dot(rows[1], down_weight, NT)], axis=1
    )
    sums = lax.psum_scatter(sums, "narrow", scatter_dimension=0, tiled=True)
    both = jnp.concatenate(
        gate_terms(sums[:, :hidden], sums[:, hidden : 2 * hidden], sums[:, 2 * hidden :]), axis=1
    )
    both = lax.all_gather(both, "narrow", axis=0, tiled=True)
    back = dot(both[:, :hidden], gate_weight, NT) + dot(both[:, hidden:], up_weight, NT)
    return lax.psum_scatter(back, "wide", scatter_dimension=0, tiled=True)


def solution(mesh):
    wide, narrow = mesh.shape["wide"], mesh.shape["narrow"]
    near, far = 1, 2

    def swap(x, axis, k):
        return lax.ppermute(x, axis, [(i, i ^ k) for i in range(mesh.shape[axis])])

    def turn(x, k):
        return lax.ppermute(x, "wide", [(i, (i + k) % wide) for i in range(wide)])

    def by_swaps(normed, target, own_target, gate_weight, up_weight, down_weight):
        width, hidden = gate_weight.shape
        share = hidden // narrow
        index = lax.axis_index("narrow").astype(jnp.int32).reshape(1)
        pair = [gate_weight, up_weight]
        diagonal = near | far
        targets = [own_target] + [swap(own_target, "wide", k) for k in range(1, wide)]
        normeds = [normed] + [swap(normed, "wide", k) for k in range(1, wide)]

        ahead = rows_ahead(index, down_weight, [near], share)
        ahead, *targets[1:] = lax.optimization_barrier((ahead, *targets[1:]))
        send, keep, held_diagonal = hidden_gradient(
            index, targets, ahead, down_weight, pair, diagonal, [near, diagonal, 0, far], share
        )
        send, *normeds = lax.optimization_barrier((send, *normeds))
        hidden_near = swap(send, "narrow", near)
        (part,) = gate_and_up(index, normeds, held_diagonal, pair, [], share, [send], "gate_up_diagonal")
        part, hidden_near = lax.optimization_barrier((part, hidden_near))
        sum_far = (keep[:, share:] + hidden_near[:, share:].astype(F32)).astype(BF16)
        hidden_far = swap(sum_far, "narrow", far)
        got = swap(part, "narrow", near)
        (part,) = gate_and_up(index, normeds, None, pair, [far], share, [sum_far], "gate_up_far", False)
        part, got, hidden_far = lax.optimization_barrier((part, got, hidden_far))
        sum_far = (part + got).astype(BF16)
        got_far = swap(sum_far, "narrow", far)
        own, part, held = gate_and_up(
            index, normeds, None, pair, [0, near], share, [sum_far], "gate_up_near_own"
        )
        part, got_far = lax.optimization_barrier((part, got_far))
        got = swap(part, "narrow", near)
        rows, held = gate_rows(own, got, got_far, keep, hidden_near, hidden_far, held)

        rows_far = swap(rows, "narrow", far)
        rows_near = swap(rows, "narrow", near)
        total, held = backward(index, [rows, rows_near], held, pair, [far], None, 1, "back_own_near")
        total, rows_far = lax.optimization_barrier((total, rows_far))
        rows_diagonal = swap(rows_far, "narrow", near)
        total, held = backward(index, [rows_far], held, pair, [diagonal], total, 1, "back_far")
        pieces = backward(index, [rows_diagonal], held, pair, [], total, wide, "back_diagonal")
        back_normed, inner = pieces[0][:, :width], pieces[0][:, width : width + 1]
        for k in reversed(range(1, wide)):
            got = swap(pieces[k], "wide", k)
            back_normed = back_normed + got[:, :width].astype(F32)
            inner = inner + joined(got[:, width:])
        return back_normed, inner

    def on_device(tokens, signs, magnitude, target, norm_gain, gate_weight, up_weight, down_weight):
        width, hidden = gate_weight.shape
        features = width * narrow
        weights = (gate_weight, up_weight, down_weight)
        square = narrow == (near | far) + 1 and hidden % (narrow * LANES) == 0 and wide & (wide - 1) == 0

        delta, latent, squares, gain, own_target = latents(
            tokens, signs, magnitude, norm_gain.reshape(1, -1), target
        )
        if square:
            squares = squares + sum(swap(squares, "narrow", k) for k in range(1, narrow))
        else:
            squares = lax.psum(squares, "narrow")
        scale = lax.rsqrt(squares / features + EPS)
        unit = latent * scale
        normed = (unit * gain).astype(BF16)
        if square:
            back_normed, inner = by_swaps(normed, target, own_target, *weights)
            scaled = back_normed * gain
        else:
            scaled = by_collectives(normed, target, *weights) * gain
            inner = lax.psum(jnp.sum(scaled * unit, axis=1, keepdims=True), "narrow")
        back_latent = scale * (scaled - unit * (inner / features))
        return delta + ASCENT * (own_target.astype(F32) + back_latent)

    rows = P(("groups", "wide"), "narrow")
    in_specs = (rows, rows, rows, rows, P("narrow"), P("narrow", "wide"), P("narrow", "wide"), P("wide", "narrow"))
    return jax.shard_map(on_device, mesh=mesh, in_specs=in_specs, out_specs=rows, check_vma=False)
```
